256 devices in a mesh: grp: 2 (over x_lo), seq: 16 (over y, x_hi, core), rep: 8 (over z).
Axes of the slice: x: 4 (x_hi: 2, x_lo: 2; x = x_hi * 2 + x_lo), y: 4, z: 8, core: 2. Of those that a mesh axis runs over, the one named last changes fastest.
Arguments:
- pre_query: bfloat16 [2, 4096, 8192], P('grp', 'seq', 'rep'), may hold values from -6 to 6
- history_key: bfloat16 [2, 2048, 1024], P('grp', 'seq', 'rep'), may hold values from -6 to 6
- history_value: bfloat16 [2, 2048, 1024], P('grp', 'seq', 'rep'), may hold values from -6 to 6
- document_key: bfloat16 [2, 4096, 1024], P('grp', 'seq', 'rep'), may hold values from -6 to 6
- document_value: bfloat16 [2, 4096, 1024], P('grp', 'seq', 'rep'), may hold values from -6 to 6
- stretch_start: int32 [2], P('grp'), may hold values from 1024 to 2048
- decode_query: bfloat16 [512, 4, 8192], P(('grp', 'rep'), None, 'seq'), may hold values from -6 to 6
- cached_row_keys: bfloat16 [512, 16, 256, 128], P(('grp', 'rep'), 'seq'), may hold values from -6 to 6
- cached_row_values: bfloat16 [512, 16, 256, 128], P(('grp', 'rep'), 'seq'), may hold values from -6 to 6
- cache_lengths: int32 [512], P(('grp', 'rep')), may hold values from 1 to 512, as said below
- doc_owner: int32 [512], P(('grp', 'rep')), may hold values from 0 to 1
- decode_key: bfloat16 [512, 4, 1024], P(('grp', 'rep')), may hold values from -6 to 6
- decode_value: bfloat16 [512, 4, 1024], P(('grp', 'rep')), may hold values from -6 to 6
Outputs:
- prefill_output: bfloat16 [2, 4096, 8192], P('grp', 'seq', 'rep')
- dec_out: bfloat16 [512, 4, 8192], P(('grp', 'rep'), None, 'seq')
The draws below stay inside these ranges and needn't reach their ends.
Inputs may be any that keep to these rules, and one draw needn't show every extreme that they name: `cache_lengths`: some row has exactly 512 valid positions.
All inputs are finite; a program needn't handle non-finite values.
Results may differ from the reference program's by a relative error of at most 0.019.
Values may be sent and summed in bfloat16 or wider, within the bound.
A program may use at most 128 MiB of HBM per device.

```python
import jax
import jax.numpy as jnp
from jax import lax

QUERY_HEADS = 64
KEY_VALUE_HEADS = 8
HEAD_SIZE = 128
GROUP_QUERIES = 8
CACHE_SLOTS = 512
DECODE_STEPS = 4
DOCUMENT_TOKENS = 4096
HISTORY_SLOTS = 2048
DIALOGUE_ROWS = 512
CACHE_RUNS = 2


def draw_document_key(key, part):
    array_shape = (2, DOCUMENT_TOKENS, KEY_VALUE_HEADS * HEAD_SIZE)
    key = jax.random.fold_in(key, 3)
    base = jnp.clip(jax.random.normal(key, array_shape, jnp.float32), -6.0, 6.0)
    return base.astype(jnp.bfloat16)


def draw_pre_query(key, part):
    key = jax.random.fold_in(key, 5)
    array_shape = (2, DOCUMENT_TOKENS, QUERY_HEADS * HEAD_SIZE)
    base = jnp.clip(jax.random.normal(key, array_shape, jnp.float32), -6.0, 6.0)
    return base.astype(jnp.bfloat16)


def draw_decode_key(key, part):
    array_shape = (DIALOGUE_ROWS, DECODE_STEPS, KEY_VALUE_HEADS * HEAD_SIZE)
    key = jax.random.fold_in(key, 7)
    base = jnp.clip(jax.random.normal(key, array_shape, jnp.float32), -6.0, 6.0)
    return base.astype(jnp.bfloat16)


def draw_decode_query(key, part):
    key = jax.random.fold_in(key, 9)
    array_shape = (DIALOGUE_ROWS, DECODE_STEPS, QUERY_HEADS * HEAD_SIZE)
    base = jnp.clip(jax.random.normal(key, array_shape, jnp.float32), -6.0, 6.0)
    return base.astype(jnp.bfloat16)


def draw_cache_lengths(key, part):
    key = jax.random.fold_in(key, 11)
    first, second = jax.random.split(key)
    drawn = jax.random.randint(first, (DIALOGUE_ROWS,), 0, CACHE_SLOTS, jnp.int32)
    lengths = 1 + drawn * drawn // CACHE_SLOTS
    chosen = jax.random.randint(second, (), 0, DIALOGUE_ROWS, jnp.int32)
    return jnp.where(jnp.arange(DIALOGUE_ROWS, dtype=jnp.int32) == chosen, CACHE_SLOTS, lengths).astype(jnp.int32)


def with_ends(entries, own_key, low, largest):
    longest = entries.shape.index(max(entries.shape))
    spots = []
    for shift in (0, 1):
        where = [jax.random.randint(jax.random.fold_in(own_key, axis), (), 0, length) for axis, length in enumerate(entries.shape)]
        where[longest] = (where[longest] + shift) % entries.shape[longest]
        spots.append(tuple(where))
    return entries.at[spots[0]].set(low).at[spots[1]].set(largest)


def levels(key, extent, pieces, low, high):
    loudness = 1.0
    for dim, blocks in pieces:
        steps = jax.random.uniform(jax.random.fold_in(jax.random.fold_in(key, 6), dim), (blocks,), jnp.float32, low / len(pieces), high / len(pieces))
        loudness = loudness * jnp.repeat(jnp.exp(steps), extent[dim] // blocks).reshape((-1,) + (1,) * (len(extent) - 1 - dim))
    return loudness


def scatter_about(stream_key, shape, spread, limit, cuts=(), held_as=jnp.bfloat16):
    array = jax.random.normal(stream_key, shape, jnp.float32) * spread
    if len(cuts) > 0:
        array = levels(stream_key, shape, cuts, -0.22, 0.18) * array
    return jnp.clip(array, min=-limit, max=limit).astype(held_as)


def setup_inputs(seed: int = 0) -> dict:
    splits = jax.random.split(jax.random.key(seed), 14)
    pre_query = draw_pre_query(jax.random.fold_in(splits[13], 71), 0)
    history_key = scatter_about(splits[1], (2, HISTORY_SLOTS, KEY_VALUE_HEADS * HEAD_SIZE), 1.0, 6.0, ((0, 2), (1, 16), (2, 8)))
    history_value = scatter_about(splits[2], (2, HISTORY_SLOTS, KEY_VALUE_HEADS * HEAD_SIZE), 1.0, 6.0, ((0, 2), (1, 16), (2, 8)))
    document_key = draw_document_key(jax.random.fold_in(splits[13], 71), 0)
    document_value = scatter_about(splits[4], (2, DOCUMENT_TOKENS, KEY_VALUE_HEADS * HEAD_SIZE), 1.0, 6.0, ((0, 2), (1, 16), (2, 8)))
    stretch_start = jax.random.randint(splits[5], (2,), HISTORY_SLOTS // 2, HISTORY_SLOTS + 1).astype(jnp.int32)
    decode_query = draw_decode_query(jax.random.fold_in(splits[13], 71), 0)
    cached_row_keys = scatter_about(splits[7], (DIALOGUE_ROWS, KEY_VALUE_HEADS * CACHE_RUNS, CACHE_SLOTS // CACHE_RUNS, HEAD_SIZE), 1.0, 6.0, ((0, 16), (1, 16)))
    cached_row_values = scatter_about(splits[8], (DIALOGUE_ROWS, KEY_VALUE_HEADS * CACHE_RUNS, CACHE_SLOTS // CACHE_RUNS, HEAD_SIZE), 1.0, 6.0, ((0, 16), (1, 16)))
    cache_lengths = draw_cache_lengths(jax.random.fold_in(splits[13], 71), 0)
    doc_owner = with_ends(jax.random.randint(splits[10], (DIALOGUE_ROWS,), 0, 2), jax.random.fold_in(splits[10], 1), 0, 1).astype(jnp.int32)
    decode_key = draw_decode_key(jax.random.fold_in(splits[13], 71), 0)
    decode_value = scatter_about(splits[12], (DIALOGUE_ROWS, DECODE_STEPS, KEY_VALUE_HEADS * HEAD_SIZE), 1.0, 6.0, ((0, 16),))
    return {"pre_query": pre_query, "history_key": history_key, "history_value": history_value, "document_key": document_key, "document_value": document_value, "stretch_start": stretch_start, "decode_query": decode_query, "cached_row_keys": cached_row_keys, "cached_row_values": cached_row_values, "cache_lengths": cache_lengths, "doc_owner": doc_owner, "decode_key": decode_key, "decode_value": decode_value}


def weighted_sum(scores, visible, value_rows, form_scores, form_values):
    masked = jnp.where(visible, scores, jnp.float32(-1e30))
    top = jnp.max(masked, axis=-1, keepdims=True)
    weights = jnp.where(visible, jnp.exp(scores - top), jnp.float32(0.0))
    total = jnp.sum(weights, axis=-1)
    rounded = weights.astype(jnp.bfloat16)
    summed = jnp.einsum(form_values, rounded.astype(jnp.float32), value_rows.astype(jnp.float32))
    return (summed / total[..., None]).astype(jnp.bfloat16)


def reference(pre_query, history_key, history_value, document_key, document_value, stretch_start, decode_query, cached_row_keys, cached_row_values, cache_lengths, doc_owner, decode_key, decode_value):
    scale = HEAD_SIZE ** -0.5
    query_block = min(DOCUMENT_TOKENS, 512)
    block_count = DOCUMENT_TOKENS // query_block
    zero_index = jnp.int32(0)

    def prefill_item(index_value):
        index_value = index_value.astype(jnp.int32)
        group_number = (index_value // (KEY_VALUE_HEADS * block_count)).astype(jnp.int32)
        head_number = ((index_value // block_count) % KEY_VALUE_HEADS).astype(jnp.int32)
        block = (index_value % block_count).astype(jnp.int32)
        row_start = (block * query_block).astype(jnp.int32)
        query_column = (head_number * (GROUP_QUERIES * HEAD_SIZE)).astype(jnp.int32)
        head_column = (head_number * HEAD_SIZE).astype(jnp.int32)
        query_rows = lax.dynamic_slice(pre_query, (group_number, row_start, query_column), (1, query_block, GROUP_QUERIES * HEAD_SIZE))[0]
        query_rows = query_rows.reshape(query_block, GROUP_QUERIES, HEAD_SIZE)
        key_rows = jnp.concatenate([lax.dynamic_slice(history_key, (group_number, zero_index, head_column), (1, HISTORY_SLOTS, HEAD_SIZE))[0],
                                lax.dynamic_slice(document_key, (group_number, zero_index, head_column), (1, DOCUMENT_TOKENS, HEAD_SIZE))[0]], axis=0)
        value_rows = jnp.concatenate([lax.dynamic_slice(history_value, (group_number, zero_index, head_column), (1, HISTORY_SLOTS, HEAD_SIZE))[0],
                                  lax.dynamic_slice(document_value, (group_number, zero_index, head_column), (1, DOCUMENT_TOKENS, HEAD_SIZE))[0]], axis=0)
        rows = row_start + jnp.arange(query_block, dtype=jnp.int32)
        slots = jnp.arange(HISTORY_SLOTS + DOCUMENT_TOKENS, dtype=jnp.int32)
        start = stretch_start[group_number]
        visible = jnp.where(slots[None, :] < HISTORY_SLOTS, slots[None, :] < start, (slots[None, :] - HISTORY_SLOTS) <= rows[:, None])
        scores = jnp.einsum('igd,kd->igk', query_rows.astype(jnp.float32), key_rows.astype(jnp.float32)) * scale
        return weighted_sum(scores, visible[:, None, :], value_rows, 'igk', 'igk,kd->igd')

    block_list = lax.map(prefill_item, jnp.arange(2 * KEY_VALUE_HEADS * block_count, dtype=jnp.int32))
    prefill_output = block_list.reshape(2, KEY_VALUE_HEADS, block_count, query_block, GROUP_QUERIES, HEAD_SIZE).transpose(0, 2, 3, 1, 4, 5).reshape(2, DOCUMENT_TOKENS, QUERY_HEADS * HEAD_SIZE)

    def dec_row(row_number):
        owning_device = doc_owner[row_number]
        length = cache_lengths[row_number]
        query_rows = decode_query[row_number].reshape(DECODE_STEPS, KEY_VALUE_HEADS, GROUP_QUERIES, HEAD_SIZE)
        document_keys = document_key[owning_device].reshape(DOCUMENT_TOKENS, KEY_VALUE_HEADS, HEAD_SIZE).transpose(1, 0, 2)
        document_values = document_value[owning_device].reshape(DOCUMENT_TOKENS, KEY_VALUE_HEADS, HEAD_SIZE).transpose(1, 0, 2)
        key_rows = jnp.concatenate([document_keys, cached_row_keys[row_number].reshape(KEY_VALUE_HEADS, CACHE_SLOTS, HEAD_SIZE),
                                decode_key[row_number].reshape(DECODE_STEPS, KEY_VALUE_HEADS, HEAD_SIZE).transpose(1, 0, 2)], axis=1)
        value_rows = jnp.concatenate([document_values, cached_row_values[row_number].reshape(KEY_VALUE_HEADS, CACHE_SLOTS, HEAD_SIZE),
                                  decode_value[row_number].reshape(DECODE_STEPS, KEY_VALUE_HEADS, HEAD_SIZE).transpose(1, 0, 2)], axis=1)
        slots = jnp.arange(DOCUMENT_TOKENS + CACHE_SLOTS + DECODE_STEPS, dtype=jnp.int32)
        steps = jnp.arange(DECODE_STEPS, dtype=jnp.int32)
        in_doc = slots < DOCUMENT_TOKENS
        in_cache = (slots >= DOCUMENT_TOKENS) & (slots < DOCUMENT_TOKENS + CACHE_SLOTS) & (slots - DOCUMENT_TOKENS < length)
        in_new = (slots >= DOCUMENT_TOKENS + CACHE_SLOTS) & ((slots - DOCUMENT_TOKENS - CACHE_SLOTS)[None, :] <= steps[:, None])
        visible = in_doc[None, :] | in_cache[None, :] | in_new
        scores = jnp.einsum('thgd,hkd->thgk', query_rows.astype(jnp.float32), key_rows.astype(jnp.float32)) * scale
        out = weighted_sum(scores, visible[:, None, None, :], value_rows, 'thgk', 'thgk,hkd->thgd')
        return out.reshape(DECODE_STEPS, QUERY_HEADS * HEAD_SIZE)

    dec_out = lax.map(dec_row, jnp.arange(DIALOGUE_ROWS, dtype=jnp.int32))
    return prefill_output, dec_out
```

```python
import functools

import jax
import jax.numpy as jnp
from jax import lax
from jax.experimental import pallas as pl
from jax.experimental.pallas import tpu as pltpu
from jax.sharding import PartitionSpec as P

HEAD = 128
LOG2E = 1.4426950408889634
SCALE = HEAD ** (-0.5) * LOG2E
LOW = -1e30
F32 = jnp.float32
BF16 = jnp.bfloat16
MESH = pl.DeviceIdType.MESH
NT = (((1,), (1,)), ((), ()))
NN = (((1,), (0,)), ((), ()))


def kernel(
    pre_query,
    hist_key,
    hist_value,
    doc_key,
    doc_value,
    start_ref,
    dec_query,
    cache_key,
    cache_value,
    length_ref,
    owner_ref,
    new_key,
    new_value,
    pre_out,
    dec_out,
    buf,
    vals,
    pre_q,
    pre_raw,
    pre_o,
    q_own,
    q_sib,
    ck,
    cv,
    kn,
    vn,
    o_own,
    l_own,
    o_snd,
    l_snd,
    o_sib,
    l_sib,
    dq,
    od_snd,
    ld_snd,
    od,
    ld,
    dec_o,
    s0,
    s1,
    s2,
    acc,
    tot,
    mrun,
    macc,
    dacc,
    dtot,
    dmrun,
    dmacc,
    in_sem,
    out_sem,
    send_sem,
    r0,
    r1,
    rx,
):
    grp = lax.axis_index("grp")
    seq = lax.axis_index("seq")
    rep = lax.axis_index("rep")
    y, xh, core = seq // 4, (seq // 2) % 2, seq % 2
    run = core
    chip = seq // 2

    def seq_at(dy, other):
        return ((y + dy) % 4) * 4 + (xh + other) % 2 * 2 + core

    up = {"seq": seq_at(1, 0)}
    down = {"seq": seq_at(3, 0)}
    across = {"seq": seq_at(0, 1)}
    sib = {"seq": seq + 1 - 2 * core}
    doc_seq = ((rep + 1) % 8) * 2 + grp
    doc_dev = [{"grp": g, "seq": doc_seq, "rep": chip} for g in range(2)]
    src_rep = (chip + 7) % 8
    src_dev = [{"grp": core, "seq": 2 * rep + i, "rep": src_rep} for i in range(2)]

    loads = [
        pltpu.make_async_copy(hist_key, buf.at[seq, pl.ds(0, 128)], in_sem.at[0]),
        pltpu.make_async_copy(doc_key, buf.at[seq, pl.ds(128, 256)], in_sem.at[1]),
        pltpu.make_async_copy(hist_value, vals.at[pl.ds(0, 128)], in_sem.at[2]),
        pltpu.make_async_copy(doc_value, vals.at[pl.ds(128, 256)], in_sem.at[3]),
        pltpu.make_async_copy(dec_query, q_own, in_sem.at[4]),
        pltpu.make_async_copy(cache_key, ck, in_sem.at[5]),
        pltpu.make_async_copy(cache_value, cv, in_sem.at[6]),
        pltpu.make_async_copy(pre_query, pre_raw, in_sem.at[7]),
        pltpu.make_async_copy(new_key, kn, in_sem.at[8]),
        pltpu.make_async_copy(new_value, vn, in_sem.at[9]),
    ]
    for c in loads:
        c.start()

    barrier = pltpu.get_barrier_semaphore()
    partners = [up, down, across, sib] + doc_dev + src_dev
    for d in partners:
        pl.semaphore_signal(barrier, inc=1, device_id=d, device_id_type=MESH)

    for c in loads[:4]:
        c.wait()
    for i in range(3):
        v = vals[i * 128 : (i + 1) * 128, :]
        buf[seq, 384 + i * 128 : 512 + i * 128, :] = v.astype(F32).T.astype(BF16)
    loads[4].wait()
    pl.semaphore_wait(barrier, len(partners))

    sends = []

    def send(src, dst, recv, dev):
        c = pltpu.make_async_remote_copy(
            src_ref=src,
            dst_ref=dst,
            send_sem=send_sem.at[len(sends)],
            recv_sem=recv,
            device_id=dev,
            device_id_type=MESH,
        )
        c.start()
        sends.append(c)

    def arrived(dst, recv):
        pltpu.make_async_remote_copy(
            src_ref=dst,
            dst_ref=dst,
            send_sem=send_sem.at[0],
            recv_sem=recv,
            device_id=sib,
            device_id_type=MESH,
        ).wait_recv()

    first, second = pl.ds(0, 384), pl.ds(384, 384)

    def send_block(b, dev):
        send(buf.at[b], buf.at[b], r0.at[b], dev)

    def send_first(b, dev):
        send(buf.at[b, first], buf.at[b, first], r0.at[b], dev)

    def send_second(b, dev):
        send(buf.at[b, second], buf.at[b, second], r1.at[b], dev)

    def block_in(b):
        arrived(buf.at[b], r0.at[b])

    def halves_in(b):
        arrived(buf.at[b, first], r0.at[b])
        arrived(buf.at[b, second], r1.at[b])

    send(q_own, q_sib, rx.at[0], sib)
    send_block(seq, across)
    send_block(seq, up)
    send_block(seq, down)
    send_block(seq, sib)
    for g in range(2):
        send(q_own, dq.at[pl.ds(run * 512, 512)], rx.at[1 + run], doc_dev[g])

    def cache_rows(group, _):
        for i in range(4):
            r = group * 4 + i
            rows = pl.ds(pl.multiple_of(r * 16, 16), 16)
            q = jnp.concatenate([q_own[rows, :], q_sib[rows, :]], axis=0)
            s = lax.dot_general(q, ck[r], NT, preferred_element_type=F32)
            at = run * 256 + lax.broadcasted_iota(jnp.int32, (32, 256), 1)
            seen = at < length_ref[r]
            s = jnp.where(seen, s, LOW)
            m = jnp.max(s, axis=1, keepdims=True)
            p = jnp.where(seen, jnp.exp2(s - m), 0.0)
            l = jnp.sum(p, axis=1, keepdims=True)
            o = lax.dot_general(p.astype(BF16), cv[r], NN, preferred_element_type=F32)
            safe = jnp.maximum(l, 1e-30)
            o = o / safe
            top = jnp.where(l > 0.0, m + jnp.log(safe) * LOG2E, LOW)
            top = jnp.broadcast_to(top, (32, 128))
            o_own[rows, :] = o[:16]
            l_own[rows, :] = top[:16]
            o_snd[rows, :] = o[16:].astype(BF16)
            l_snd[rows, :] = top[16:]
        return 0

    arrived(q_sib, rx.at[0])
    loads[5].wait()
    loads[6].wait()
    lax.fori_loop(0, 4, cache_rows, 0)

    block_in(seq_at(0, 1))
    send_block(seq_at(0, 1), up)
    send_block(seq_at(0, 1), down)
    send_block(seq_at(0, 1), sib)
    block_in(seq_at(3, 0))
    send_first(seq_at(3, 0), up)
    send_block(seq_at(3, 0), sib)
    block_in(seq_at(1, 0))
    send_second(seq_at(1, 0), down)
    send_block(seq_at(1, 0), sib)

    lax.fori_loop(4, 8, cache_rows, 0)
    send(o_snd, o_sib, rx.at[3], sib)
    send(l_snd, l_sib, rx.at[4], sib)

    loads[7].wait()
    for h in range(8):
        x = pre_raw[:, h * 128 : (h + 1) * 128].astype(F32) * SCALE
        pre_q[h * 256 : (h + 1) * 256, :] = x.astype(BF16)

    acc[...] = jnp.zeros_like(acc)
    tot[...] = jnp.zeros_like(tot)
    mrun[...] = jnp.full_like(mrun, LOW)
    macc[...] = jnp.full_like(macc, LOW)

    def hist_keys(row):
        return jnp.concatenate([buf[row * 4 + c, 0:128, :] for c in range(4)], axis=0)

    def hist_vals(row):
        return jnp.concatenate([buf[row * 4 + c, 384:512, :] for c in range(4)], axis=1)

    def doc_keys(c):
        return jnp.concatenate([buf[c * 2 + i, 128:384, :] for i in range(2)], axis=0)

    def doc_vals(c):
        parts = [buf[c * 2 + i, 512 + 128 * j : 640 + 128 * j, :] for i in range(2) for j in range(2)]
        return jnp.concatenate(parts, axis=1)

    def score(q, keys, out, top, mask=None):
        lanes = q.shape[0]
        s = lax.dot_general(keys, q[...], NT, preferred_element_type=F32)
        if mask is not None:
            s = mask(s)
        out[:, :lanes] = s
        return jnp.maximum(top, jnp.max(s.reshape(64, 8, lanes), axis=0))

    def weigh(s, vals_t, m, state):
        a, t, ma = state
        lanes = a.shape[1]
        now = jnp.max(m, axis=0, keepdims=True)
        before = jnp.max(ma[...], axis=0, keepdims=True)
        f = jnp.exp2(before - now)
        p = jnp.exp2(s[:, :lanes] - now)
        t[...] = t[...] * f + jnp.sum(p.reshape(64, 8, lanes), axis=0)
        a[...] = a[...] * f + lax.dot_general(
            vals_t, p.astype(BF16), NN, preferred_element_type=F32
        )
        ma[...] = m

    pre_state = (acc, tot, macc)

    def hist_mask(row):
        def mask(s):
            slot = row * 512 + lax.broadcasted_iota(jnp.int32, (512, 128), 0)
            bias = jnp.where(slot < start_ref[0], 0.0, LOW)
            return s + jnp.concatenate([bias] * 16, axis=1)

        return mask

    def causal_mask(s):
        key_at = lax.broadcasted_iota(jnp.int32, s.shape, 0)
        query_at = core * 256 + (lax.broadcasted_iota(jnp.int32, s.shape, 1) & 255)
        return jnp.where(key_at <= query_at, s, LOW)

    def step(keys, out, mask, s, vals_t):
        m = mrun[...]
        new = score(pre_q, keys, out, m, mask)
        weigh(s, vals_t, m, pre_state)
        mrun[...] = new

    block_in(seq + 1 - 2 * core)
    mrun[...] = score(pre_q, doc_keys(chip), s1, mrun[...], causal_mask)
    block_in(((y * 4) + (1 - xh) * 2) + 1 - core)

    @pl.when(xh == 1)
    def _():
        step(doc_keys(y * 2), s2, None, s1, doc_vals(chip))
        step(hist_keys(y), s0, hist_mask(y), s2, doc_vals(y * 2))

    @pl.when(xh == 0)
    def _():
        step(hist_keys(y), s0, hist_mask(y), s1, doc_vals(chip))

    block_in(seq_at(3, 1))
    send_first(seq_at(3, 1), up)
    send_block(seq_at(3, 1), sib)
    block_in(seq_at(1, 1))
    send_second(seq_at(1, 1), down)
    send_block(seq_at(1, 1), sib)

    def other_in(row):
        for x in range(2):
            block_in(row * 4 + x * 2 + 1 - core)

    def row_step(row, last):
        @pl.when(row < y)
        def _():
            step(doc_keys(row * 2), s1, None, s0, hist_vals(last))
            step(doc_keys(row * 2 + 1), s2, None, s1, doc_vals(row * 2))
            step(hist_keys(row), s0, hist_mask(row), s2, doc_vals(row * 2 + 1))

        @pl.when(row > y)
        def _():
            weigh(s0, hist_vals(last), mrun[...], pre_state)
            mrun[...] = score(pre_q, hist_keys(row), s0, mrun[...], hist_mask(row))

    def row_of(k):
        return (y + jnp.where(k == 0, 0, jnp.where(k == 1, 3, k - 1))) % 4

    def near_row(k, _):
        row = row_of(k)
        other_in(row)
        row_step(row, row_of(k - 1))
        return 0

    lax.fori_loop(1, 3, near_row, 0)

    for x in range(2):
        halves_in(seq_at(2, x))
        send_block(seq_at(2, x), sib)
    other_in((y + 2) % 4)

    for i in range(2):
        arrived(dq.at[pl.ds(i * 512, 512)], rx.at[1 + i])
    dec_state = (dacc, dtot, dmacc)
    dacc[...] = jnp.zeros_like(dacc)
    dtot[...] = jnp.zeros_like(dtot)
    dmacc[...] = jnp.full_like(dmacc, LOW)
    dmrun[...] = score(dq, doc_keys(0), s1, jnp.full(dmrun.shape, LOW, F32))

    def doc_pair(j, _):
        m = dmrun[...]
        new = score(dq, doc_keys(2 * j + 1), s2, m)
        weigh(s1, doc_vals(2 * j), m, dec_state)
        last = score(dq, doc_keys((2 * j + 2) % 8), s1, new)
        weigh(s2, doc_vals(2 * j + 1), new, dec_state)
        dmrun[...] = last
        return 0

    lax.fori_loop(0, 4, doc_pair, 0)
    total = jnp.sum(dtot[...], axis=0, keepdims=True)
    level = jnp.max(dmacc[...], axis=0, keepdims=True) + jnp.log(total) * LOG2E
    level = jnp.broadcast_to(level, (8, 1024))
    for i in range(2):
        ld_snd[i] = level[:, i * 512 : (i + 1) * 512]
    od_snd[...] = (dacc[...] / total).T.astype(BF16)
    for i in range(2):
        send(od_snd.at[pl.ds(i * 512, 512)], od.at[grp], rx.at[5 + grp], src_dev[i])
        send(ld_snd.at[i], ld.at[grp], rx.at[7 + grp], src_dev[i])

    row_step((y + 2) % 4, (y + 1) % 4)
    weigh(s0, hist_vals((y + 2) % 4), mrun[...], pre_state)
    total = jnp.sum(tot[...], axis=0, keepdims=True)
    for h in range(8):
        cols = slice(h * 256, (h + 1) * 256)
        o = acc[:, cols] / total[:, cols]
        pre_o[:, h * 128 : (h + 1) * 128] = o.T.astype(BF16)
    pre_copy = pltpu.make_async_copy(pre_o, pre_out, out_sem.at[0])
    pre_copy.start()

    loads[8].wait()
    loads[9].wait()
    arrived(o_sib, rx.at[3])
    arrived(l_sib, rx.at[4])
    for g in range(2):
        arrived(od.at[g], rx.at[5 + g])
        arrived(ld.at[g], rx.at[7 + g])
    for c in range(4):
        rows = slice(c * 128, (c + 1) * 128)
        own_doc = jnp.concatenate(
            [jnp.full((16, 128), owner_ref[c * 8 + i], jnp.int32) for i in range(8)], axis=0
        )
        is_first = own_doc == 0
        levels = [jnp.broadcast_to(ld[g, 0:1, rows], (128, 128)).T for g in range(2)]
        l_doc = jnp.where(is_first, levels[0], levels[1])
        o_doc = jnp.where(is_first, od[0, rows, :].astype(F32), od[1, rows, :].astype(F32))
        s = lax.dot_general(q_own[rows, :], kn[...], NT, preferred_element_type=F32)
        line = c * 128 + lax.broadcasted_iota(jnp.int32, (128, 128), 0)
        col = lax.broadcasted_iota(jnp.int32, (128, 128), 1)
        seen = ((line >> 4) == (col >> 2)) & ((col & 3) <= ((line >> 2) & 3))
        s = jnp.where(seen, s, LOW)
        m = jnp.max(s, axis=1, keepdims=True)
        top = jnp.maximum(jnp.maximum(l_doc, l_own[rows, :]), jnp.maximum(l_sib[rows, :], m))
        p = jnp.where(seen, jnp.exp2(s - top), 0.0)
        w_doc = jnp.exp2(l_doc - top)
        w_own = jnp.exp2(l_own[rows, :] - top)
        w_sib = jnp.exp2(l_sib[rows, :] - top)
        o = lax.dot_general(p.astype(BF16), vn[...], NN, preferred_element_type=F32)
        o = o + w_doc * o_doc + w_own * o_own[rows, :] + w_sib * o_sib[rows, :].astype(F32)
        weight = jnp.sum(p, axis=1, keepdims=True) + w_doc + w_own + w_sib
        dec_o[rows, :] = (o / weight).astype(BF16)
    dec_copy = pltpu.make_async_copy(dec_o, dec_out, out_sem.at[1])
    dec_copy.start()
    for c in sends:
        c.wait_send()
    pre_copy.wait()
    dec_copy.wait()


def local(
    pre_query,
    history_key,
    history_value,
    document_key,
    document_value,
    stretch_start,
    decode_query,
    cached_row_keys,
    cached_row_values,
    cache_lengths,
    doc_owner,
    decode_key,
    decode_value,
):
    seq = lax.axis_index("seq")
    scaled = (decode_query.reshape(32, 4, 4, HEAD).astype(F32) * SCALE).astype(BF16)
    dec_q = scaled.reshape(512, HEAD)
    at = seq // 2 * HEAD
    new_key = lax.dynamic_slice_in_dim(decode_key, at, HEAD, 2).reshape(128, HEAD)
    new_value = lax.dynamic_slice_in_dim(decode_value, at, HEAD, 2).reshape(128, HEAD)
    smem = pl.BlockSpec(memory_space=pltpu.SMEM)
    hbm = pl.BlockSpec(memory_space=pl.ANY)

    def vm(shape, dtype):
        return pltpu.VMEM(shape, dtype)

    pre, dec = pl.pallas_call(
        kernel,
        out_shape=(
            jax.ShapeDtypeStruct((256, 1024), BF16),
            jax.ShapeDtypeStruct((512, 128), BF16),
        ),
        in_specs=[hbm, hbm, hbm, hbm, hbm, smem, hbm, hbm, hbm, smem, smem, hbm, hbm],
        out_specs=(hbm, hbm),
        scratch_shapes=[
            vm((16, 768, 128), BF16),
            vm((384, 128), BF16),
            vm((2048, 128), BF16),
            vm((256, 1024), BF16),
            vm((256, 1024), BF16),
            vm((512, 128), BF16),
            vm((512, 128), BF16),
            vm((32, 256, 128), BF16),
            vm((32, 256, 128), BF16),
            vm((128, 128), BF16),
            vm((128, 128), BF16),
            vm((512, 128), F32),
            vm((512, 128), F32),
            vm((512, 128), BF16),
            vm((512, 128), F32),
            vm((512, 128), BF16),
            vm((512, 128), F32),
            vm((1024, 128), BF16),
            vm((1024, 128), BF16),
            vm((2, 8, 512), F32),
            vm((2, 512, 128), BF16),
            vm((2, 8, 512), F32),
            vm((512, 128), BF16),
            vm((512, 2048), F32),
            vm((512, 2048), F32),
            vm((512, 2048), F32),
            vm((128, 2048), F32),
            vm((8, 2048), F32),
            vm((8, 2048), F32),
            vm((8, 2048), F32),
            vm((128, 1024), F32),
            vm((8, 1024), F32),
            vm((8, 1024), F32),
            vm((8, 1024), F32),
            pltpu.SemaphoreType.DMA((10,)),
            pltpu.SemaphoreType.DMA((2,)),
            pltpu.SemaphoreType.DMA((32,)),
            pltpu.SemaphoreType.DMA((16,)),
            pltpu.SemaphoreType.DMA((16,)),
            pltpu.SemaphoreType.DMA((9,)),
        ],
        compiler_params=pltpu.CompilerParams(
            collective_id=0, has_side_effects=True, vmem_limit_bytes=56 * 1024 * 1024
        ),
        name="attention",
    )(
        pre_query[0],
        history_key[0],
        history_value[0],
        document_key[0],
        document_value[0],
        stretch_start,
        dec_q,
        cached_row_keys.reshape(32, 256, HEAD),
        cached_row_values.reshape(32, 256, HEAD),
        cache_lengths,
        doc_owner,
        new_key,
        new_value,
    )
    return pre[None], dec.reshape(32, 4, 512)


def solution(mesh):
    placed = (
        P("grp", "seq", "rep"),
        P("grp", "seq", "rep"),
        P("grp", "seq", "rep"),
        P("grp", "seq", "rep"),
        P("grp", "seq", "rep"),
        P("grp"),
        P(("grp", "rep"), None, "seq"),
        P(("grp", "rep"), "seq", None, None),
        P(("grp", "rep"), "seq", None, None),
        P(("grp", "rep")),
        P(("grp", "rep")),
        P(("grp", "rep"), None, None),
        P(("grp", "rep"), None, None),
    )
    return jax.shard_map(
        local,
        mesh=mesh,
        in_specs=placed,
        out_specs=(P("grp", "seq", "rep"), P(("grp", "rep"), None, "seq")),
        check_vma=False,
    )
```

```python
import functools

import jax
import jax.numpy as jnp
from jax import lax
from jax.experimental import pallas as pl
from jax.experimental.pallas import tpu as pltpu
from jax.sharding import PartitionSpec as P

HEAD = 128
LOG2E = 1.4426950408889634
SCALE = HEAD ** (-0.5) * LOG2E
LOW = -1e30
F32 = jnp.float32
BF16 = jnp.bfloat16
MESH = pl.DeviceIdType.MESH
NT = (((1,), (1,)), ((), ()))
NN = (((1,), (0,)), ((), ()))


def kernel(
    pre_query,
    hist_key,
    hist_value,
    doc_key,
    doc_value,
    start_ref,
    dec_query,
    cache_key,
    cache_value,
    length_ref,
    owner_ref,
    new_key,
    new_value,
    pre_out,
    dec_out,
    buf,
    vals,
    pre_q,
    pre_raw,
    pre_o,
    q_own,
    q_sib,
    ck,
    cv,
    kn,
    vn,
    o_own,
    l_own,
    o_snd,
    l_snd,
    o_sib,
    l_sib,
    dq,
    od_snd,
    od,
    oc,
    of,
    lt,
    qa,
    dec_o,
    s1,
    s2,
    d1,
    d2,
    acc,
    tot,
    mrun,
    macc,
    dacc,
    dtot,
    dmrun,
    dmacc,
    in_sem,
    out_sem,
    send_sem,
    r0,
    r1,
    r2,
    r3,
    rx,
    ra,
    rq,
    ro,
    rf,
    own_sem,
):
    grp = lax.axis_index("grp")
    seq = lax.axis_index("seq")
    rep = lax.axis_index("rep")
    y, xh, core = seq // 4, (seq // 2) % 2, seq % 2
    run = core
    chip = seq // 2

    def seq_at(dy, other):
        return ((y + dy) % 4) * 4 + (xh + other) % 2 * 2 + core

    up = {"seq": seq_at(1, 0)}
    down = {"seq": seq_at(3, 0)}
    across = {"seq": seq_at(0, 1)}
    sib = {"seq": seq + 1 - 2 * core}
    own_slot = grp * 8 + rep
    plane = [((chip + k) % 8, {"seq": (chip + k) % 8 * 2 + core}) for k in range(8)]
    column = []
    for k in range(16):
        slot = (own_slot + k) % 16
        column.append((slot, {"grp": slot // 8, "rep": slot % 8}))

    loads = [
        pltpu.make_async_copy(hist_key, buf.at[seq, pl.ds(512, 128)], in_sem.at[0]),
        pltpu.make_async_copy(doc_key, buf.at[seq, pl.ds(0, 256)], in_sem.at[1]),
        pltpu.make_async_copy(hist_value, vals.at[pl.ds(0, 128)], in_sem.at[2]),
        pltpu.make_async_copy(doc_value, vals.at[pl.ds(128, 256)], in_sem.at[3]),
        pltpu.make_async_copy(dec_query, q_own, in_sem.at[4]),
        pltpu.make_async_copy(cache_key, ck, in_sem.at[5]),
        pltpu.make_async_copy(cache_value, cv, in_sem.at[6]),
        pltpu.make_async_copy(pre_query, pre_raw, in_sem.at[7]),
        pltpu.make_async_copy(new_key, kn, in_sem.at[8]),
        pltpu.make_async_copy(new_value, vn, in_sem.at[9]),
    ]
    for c in loads:
        c.start()

    barrier = pltpu.get_barrier_semaphore()
    partners = [sib] + [p[1] for p in plane[1:]] + [p[1] for p in column[1:]]
    for d in partners:
        pl.semaphore_signal(barrier, inc=1, device_id=d, device_id_type=MESH)

    for c in loads[:4]:
        c.wait()
    for i, at in ((0, 640), (1, 256), (2, 384)):
        v = vals[i * 128 : (i + 1) * 128, :]
        buf[seq, at : at + 128, :] = v.astype(F32).T.astype(BF16)
    loads[4].wait()
    pl.semaphore_wait(barrier, len(partners))

    sends = []

    def send(src, dst, recv, dev):
        c = pltpu.make_async_remote_copy(
            src_ref=src,
            dst_ref=dst,
            send_sem=send_sem.at[len(sends)],
            recv_sem=recv,
            device_id=dev,
            device_id_type=MESH,
        )
        c.start()
        sends.append(c)

    def arrived(dst, recv):
        pltpu.make_async_remote_copy(
            src_ref=dst,
            dst_ref=dst,
            send_sem=send_sem.at[0],
            recv_sem=recv,
            device_id=sib,
            device_id_type=MESH,
        ).wait_recv()

    class Part:
        def __init__(self, at, size, sem_a, sem_b):
            self.whole = pl.ds(at, size)
            self.first = pl.ds(at, size // 2)
            self.second = pl.ds(at + size // 2, size // 2)
            self.sem_a, self.sem_b = sem_a, sem_b

        def send(self, b, *devs):
            for dev in devs:
                ref = buf.at[b, self.whole]
                send(ref, ref, self.sem_a.at[b], dev)

        def send_first(self, b, *devs):
            for dev in devs:
                ref = buf.at[b, self.first]
                send(ref, ref, self.sem_a.at[b], dev)

        def send_second(self, b, *devs):
            for dev in devs:
                ref = buf.at[b, self.second]
                send(ref, ref, self.sem_b.at[b], dev)

        def wait(self, b):
            arrived(buf.at[b, self.whole], self.sem_a.at[b])

        def wait_first(self, b):
            arrived(buf.at[b, self.first], self.sem_a.at[b])

        def wait_second(self, b):
            arrived(buf.at[b, self.second], self.sem_b.at[b])

        def wait_sib(self, row):
            for x in range(2):
                self.wait(row * 4 + x * 2 + 1 - core)

    doc = Part(0, 512, r0, r1)
    hist = Part(512, 256, r2, r3)
    far, below, above = seq_at(0, 1), seq_at(3, 0), seq_at(1, 0)
    far_below, far_above = seq_at(3, 1), seq_at(1, 1)

    send(q_own, q_sib, rx.at[0], sib)
    doc.send_first(seq, across)
    doc.send_second(seq, across)
    doc.send(seq, up, down, sib)

    def piece(ref, i):
        return ref.at[pl.ds(pl.multiple_of(i * 64, 64), 64)]

    own_copies = [
        pltpu.make_async_copy(piece(q_own, chip), qa.at[chip], own_sem.at[0]),
        pltpu.make_async_copy(qa.at[rep], piece(dq, own_slot), own_sem.at[1]),
        pltpu.make_async_copy(od_snd.at[own_slot], od.at[own_slot], own_sem.at[2]),
    ]
    own_copies[0].start()
    for j, dev in plane[1:]:
        send(piece(q_own, j), qa.at[chip], ra.at[chip], dev)

    def cache_rows(group):
        for i in range(8):
            r = group * 8 + i
            rows = pl.ds(r * 16, 16)
            q = jnp.concatenate([q_own[rows, :], q_sib[rows, :]], axis=0)
            s = lax.dot_general(q, ck[r], NT, preferred_element_type=F32)
            at = run * 256 + lax.broadcasted_iota(jnp.int32, (32, 256), 1)
            seen = at < length_ref[r]
            s = jnp.where(seen, s, LOW)
            m = jnp.max(s, axis=1, keepdims=True)
            p = jnp.where(seen, jnp.exp2(s - m), 0.0)
            l = jnp.sum(p, axis=1, keepdims=True)
            o = lax.dot_general(p.astype(BF16), cv[r], NN, preferred_element_type=F32)
            safe = jnp.maximum(l, 1e-30)
            o = o / safe
            top = jnp.where(l > 0.0, m + jnp.log(safe) * LOG2E, LOW)
            top = jnp.broadcast_to(top, (32, 128))
            o_own[rows, :] = o[:16]
            l_own[rows, :] = top[:16]
            o_snd[rows, :] = o[16:].astype(BF16)
            l_snd[rows, :] = top[16:]

    arrived(q_sib, rx.at[0])
    loads[5].wait()
    loads[6].wait()
    cache_rows(0)

    doc.wait_first(far)
    doc.send_first(far, up, down)
    doc.wait(below)
    doc.send_first(below, up)
    doc.send(below, sib)
    doc.wait(above)
    doc.send_second(above, down)
    doc.send(above, sib)
    cache_rows(1)
    doc.wait_second(far)
    doc.send_second(far, up, down)
    doc.send(far, sib)
    hist.send_first(seq, across)
    hist.send_second(seq, across)
    hist.send(seq, up, down, sib)

    own_copies[0].wait()
    for j, _ in plane[1:]:
        arrived(qa.at[j], ra.at[j])
    own_copies[1].start()
    for slot, dev in column[1:]:
        send(qa.at[slot % 8], piece(dq, own_slot), rq.at[own_slot], dev)
    cache_rows(2)
    doc.wait_first(far_below)
    doc.send_first(far_below, up)
    doc.wait_second(far_above)
    doc.send_second(far_above, down)
    cache_rows(3)
    send(o_snd, o_sib, rx.at[3], sib)
    send(l_snd, l_sib, rx.at[4], sib)

    doc.wait_second(far_below)
    doc.send(far_below, sib)
    doc.wait_first(far_above)
    doc.send(far_above, sib)
    hist.wait_first(far)
    hist.send_first(far, up, down)
    hist.wait(below)
    hist.send_first(below, up)
    hist.send(below, sib)
    hist.wait(above)
    hist.send_second(above, down)
    hist.send(above, sib)
    hist.wait_second(far)
    hist.send_second(far, up, down)
    hist.send(far, sib)

    loads[7].wait()
    for h in range(8):
        x = pre_raw[:, h * 128 : (h + 1) * 128].astype(F32) * SCALE
        pre_q[h * 256 : (h + 1) * 256, :] = x.astype(BF16)

    acc[...] = jnp.zeros_like(acc)
    tot[...] = jnp.zeros_like(tot)
    mrun[...] = jnp.full_like(mrun, LOW)
    macc[...] = jnp.full_like(macc, LOW)

    def hist_keys(row):
        return jnp.concatenate([buf[row * 4 + c, 512:640, :] for c in range(4)], axis=0)

    def hist_vals(row):
        return jnp.concatenate([buf[row * 4 + c, 640:768, :] for c in range(4)], axis=1)

    def doc_keys(c):
        return jnp.concatenate([buf[c * 2 + i, 0:256, :] for i in range(2)], axis=0)

    def doc_vals(c):
        parts = [buf[c * 2 + i, 256 + 128 * j : 384 + 128 * j, :] for i in range(2) for j in range(2)]
        return jnp.concatenate(parts, axis=1)

    def score(q, keys, out, top, mask=None):
        lanes = q.shape[0]
        s = lax.dot_general(keys, q[...], NT, preferred_element_type=F32)
        if mask is not None:
            s = mask(s)
        out[:, :lanes] = s
        return jnp.maximum(top, jnp.max(s.reshape(64, 8, lanes), axis=0))

    def weigh(s, vals_t, m, state):
        a, t, ma = state
        lanes = a.shape[1]
        now = jnp.max(m, axis=0, keepdims=True)
        before = jnp.max(ma[...], axis=0, keepdims=True)
        f = jnp.exp2(before - now)
        p = jnp.exp2(s[:, :lanes] - now)
        t[...] = t[...] * f + jnp.sum(p.reshape(64, 8, lanes), axis=0)
        a[...] = a[...] * f + lax.dot_general(
            vals_t, p.astype(BF16), NN, preferred_element_type=F32
        )
        ma[...] = m

    pre_state = (acc, tot, macc)

    def hist_mask(row):
        def mask(s):
            slot = row * 512 + lax.broadcasted_iota(jnp.int32, (512, 128), 0)
            bias = jnp.where(slot < start_ref[0], 0.0, LOW)
            return s + jnp.concatenate([bias] * 16, axis=1)

        return mask

    def causal_mask(s):
        key_at = lax.broadcasted_iota(jnp.int32, s.shape, 0)
        query_at = core * 256 + (lax.broadcasted_iota(jnp.int32, s.shape, 1) & 255)
        return jnp.where(key_at <= query_at, s, LOW)

    def step(keys, out, mask, s, vals_t):
        m = mrun[...]
        new = score(pre_q, keys, out, m, mask)
        weigh(s, vals_t, m, pre_state)
        mrun[...] = new

    doc.wait_sib(y)

    @pl.when(xh == 1)
    def _():
        mrun[...] = score(pre_q, doc_keys(chip), s1, mrun[...], causal_mask)
        step(doc_keys(y * 2), s2, None, s1, doc_vals(chip))

    @pl.when(xh == 0)
    def _():
        mrun[...] = score(pre_q, doc_keys(chip), s2, mrun[...], causal_mask)

    for x in range(2):
        b = seq_at(2, x)
        doc.wait_first(b)
        doc.wait_second(b)
        doc.send(b, sib)
    hist.wait_first(far_below)
    hist.send_first(far_below, up)
    hist.wait_second(far_above)
    hist.send_second(far_above, down)
    hist.wait_second(far_below)
    hist.send(far_below, sib)
    hist.wait_first(far_above)
    hist.send(far_above, sib)

    def row_of(k):
        return (y + jnp.where(k == 0, 0, jnp.where(k == 1, 3, k - 1))) % 4

    def row_step(k, waiting):
        row = row_of(k)
        doc.wait_sib(row)

        @pl.when(row < y)
        def _():
            step(doc_keys(row * 2), s1, None, s2, doc_vals(waiting))
            step(doc_keys(row * 2 + 1), s2, None, s1, doc_vals(row * 2))

        return jnp.where(row < y, row * 2 + 1, waiting)

    waiting = lax.fori_loop(1, 3, row_step, y * 2)
    for x in range(2):
        b = seq_at(2, x)
        hist.wait_first(b)
        hist.wait_second(b)
        hist.send(b, sib)
    row = (y + 2) % 4
    doc.wait_sib(row)

    own_copies[1].wait()
    for slot, _ in column[1:]:
        arrived(piece(dq, slot), rq.at[slot])
    dec_state = (dacc, dtot, dmacc)
    dacc[...] = jnp.zeros_like(dacc)
    dtot[...] = jnp.zeros_like(dtot)
    dmacc[...] = jnp.full_like(dmacc, LOW)
    dmrun[...] = score(dq, doc_keys(0), d1, jnp.full(dmrun.shape, LOW, F32))

    def doc_pair(j, _):
        m = dmrun[...]
        new = score(dq, doc_keys(2 * j + 1), d2, m)
        weigh(d1, doc_vals(2 * j), m, dec_state)
        last = score(dq, doc_keys((2 * j + 2) % 8), d1, new)
        weigh(d2, doc_vals(2 * j + 1), new, dec_state)
        dmrun[...] = last
        return 0

    lax.fori_loop(0, 4, doc_pair, 0)
    total = jnp.sum(dtot[...], axis=0, keepdims=True)
    level = jnp.max(dmacc[...], axis=0, keepdims=True) + jnp.log(total) * LOG2E
    od_snd[:, 0:64, :] = (dacc[...] / total).T.astype(BF16).reshape(16, 64, 128)
    line = lax.broadcasted_iota(jnp.int32, (16, 128), 0)
    for k in range(8):
        whole = level[:, k * 128 : (k + 1) * 128]
        high = whole.astype(BF16).astype(F32)
        mid = (whole - high).astype(BF16).astype(F32)
        low = whole - high - mid
        three = jnp.where(line == 0, high, jnp.where(line == 1, mid, jnp.where(line == 2, low, 0.0)))
        for i in range(2):
            od_snd[2 * k + i, 64:80, :] = three.astype(BF16)
    own_copies[2].start()
    for slot, dev in column[1:]:
        send(od_snd.at[slot], od.at[own_slot], ro.at[own_slot], dev)

    @pl.when(row < y)
    def _():
        step(doc_keys(row * 2), s1, None, s2, doc_vals(waiting))
        step(doc_keys(row * 2 + 1), s2, None, s1, doc_vals(row * 2))

    waiting = jnp.where(row < y, row * 2 + 1, waiting)

    def hist_pair(a, b, vals_t):
        hist.wait_sib(a)
        hist.wait_sib(b)
        step(hist_keys(a), s1, hist_mask(a), s2, vals_t)
        step(hist_keys(b), s2, hist_mask(b), s1, hist_vals(a))

    hist_pair(y, (y + 3) % 4, doc_vals(waiting))

    own_copies[2].wait()
    for slot, _ in column[1:]:
        arrived(od.at[slot], ro.at[slot])
    owners = [owner_ref[chip * 4 + i] for i in range(4)]
    rows_owner = jnp.concatenate([jnp.full((16, 128), o, jnp.int32) for o in owners], axis=0)
    lane = (lax.broadcasted_iota(jnp.int32, (16, 128), 1) >> 4) & 3
    lane_owner = jnp.where(
        lane == 0, owners[0], jnp.where(lane == 1, owners[1], jnp.where(lane == 2, owners[2], owners[3]))
    )
    which = jnp.concatenate([rows_owner, lane_owner], axis=0) == 0
    for h in range(8):
        chosen = jnp.where(which, od[h].astype(F32), od[8 + h].astype(F32))
        oc[h] = chosen.astype(BF16)
    of[chip] = oc[chip]
    for h, dev in plane[1:]:
        send(oc.at[h], of.at[chip], rf.at[chip], dev)

    hist_pair((y + 1) % 4, row, hist_vals((y + 3) % 4))
    weigh(s2, hist_vals(row), mrun[...], pre_state)
    total = jnp.sum(tot[...], axis=0, keepdims=True)
    for h in range(8):
        cols = slice(h * 256, (h + 1) * 256)
        o = acc[:, cols] / total[:, cols]
        pre_o[:, h * 128 : (h + 1) * 128] = o.T.astype(BF16)
    pre_copy = pltpu.make_async_copy(pre_o, pre_out, out_sem.at[0])
    pre_copy.start()

    loads[8].wait()
    loads[9].wait()
    arrived(o_sib, rx.at[3])
    arrived(l_sib, rx.at[4])
    for j, _ in plane[1:]:
        arrived(of.at[j], rf.at[j])
    sums = [jnp.sum(of[j, 64:80, :].astype(F32), axis=0, keepdims=True) for j in range(8)]
    lt[...] = jnp.concatenate(sums * 16, axis=0).T
    levels = lt[pl.ds(pl.multiple_of(rep % 2 * 64, 64), 64), :]
    for c in range(4):
        rows = slice(c * 128, (c + 1) * 128)
        l_doc = jnp.concatenate(
            [jnp.broadcast_to(levels[:, j : j + 1], (64, 128)) for j in (2 * c, 2 * c + 1)], axis=0
        )
        o_doc = jnp.concatenate([of[j, 0:64, :].astype(F32) for j in (2 * c, 2 * c + 1)], axis=0)
        s = lax.dot_general(q_own[rows, :], kn[...], NT, preferred_element_type=F32)
        line = c * 128 + lax.broadcasted_iota(jnp.int32, (128, 128), 0)
        col = lax.broadcasted_iota(jnp.int32, (128, 128), 1)
        seen = ((line >> 4) == (col >> 2)) & ((col & 3) <= ((line >> 2) & 3))
        s = jnp.where(seen, s, LOW)
        m = jnp.max(s, axis=1, keepdims=True)
        top = jnp.maximum(jnp.maximum(l_doc, l_own[rows, :]), jnp.maximum(l_sib[rows, :], m))
        p = jnp.where(seen, jnp.exp2(s - top), 0.0)
        w_doc = jnp.exp2(l_doc - top)
        w_own = jnp.exp2(l_own[rows, :] - top)
        w_sib = jnp.exp2(l_sib[rows, :] - top)
        o = lax.dot_general(p.astype(BF16), vn[...], NN, preferred_element_type=F32)
        o = o + w_doc * o_doc + w_own * o_own[rows, :] + w_sib * o_sib[rows, :].astype(F32)
        weight = jnp.sum(p, axis=1, keepdims=True) + w_doc + w_own + w_sib
        dec_o[rows, :] = (o / weight).astype(BF16)
    dec_copy = pltpu.make_async_copy(dec_o, dec_out, out_sem.at[1])
    dec_copy.start()
    for c in sends:
        c.wait_send()
    pre_copy.wait()
    dec_copy.wait()


def local(
    pre_query,
    history_key,
    history_value,
    document_key,
    document_value,
    stretch_start,
    decode_query,
    cached_row_keys,
    cached_row_values,
    cache_lengths,
    doc_owner,
    decode_key,
    decode_value,
):
    seq = lax.axis_index("seq")
    scaled = (decode_query.reshape(32, 4, 4, HEAD).astype(F32) * SCALE).astype(BF16)
    dec_q = scaled.reshape(512, HEAD)
    at = seq // 2 * HEAD
    new_key = lax.dynamic_slice_in_dim(decode_key, at, HEAD, 2).reshape(128, HEAD)
    new_value = lax.dynamic_slice_in_dim(decode_value, at, HEAD, 2).reshape(128, HEAD)
    smem = pl.BlockSpec(memory_space=pltpu.SMEM)
    hbm = pl.BlockSpec(memory_space=pl.ANY)

    def vm(shape, dtype):
        return pltpu.VMEM(shape, dtype)

    pre, dec = pl.pallas_call(
        kernel,
        out_shape=(
            jax.ShapeDtypeStruct((256, 1024), BF16),
            jax.ShapeDtypeStruct((512, 128), BF16),
        ),
        in_specs=[hbm, hbm, hbm, hbm, hbm, smem, hbm, hbm, hbm, smem, smem, hbm, hbm],
        out_specs=(hbm, hbm),
        scratch_shapes=[
            vm((16, 768, 128), BF16),
            vm((384, 128), BF16),
            vm((2048, 128), BF16),
            vm((256, 1024), BF16),
            vm((256, 1024), BF16),
            vm((512, 128), BF16),
            vm((512, 128), BF16),
            vm((32, 256, 128), BF16),
            vm((32, 256, 128), BF16),
            vm((128, 128), BF16),
            vm((128, 128), BF16),
            vm((512, 128), F32),
            vm((512, 128), F32),
            vm((512, 128), BF16),
            vm((512, 128), F32),
            vm((512, 128), BF16),
            vm((512, 128), F32),
            vm((1024, 128), BF16),
            vm((16, 80, 128), BF16),
            vm((16, 80, 128), BF16),
            vm((8, 80, 128), BF16),
            vm((8, 80, 128), BF16),
            vm((128, 128), F32),
            vm((8, 64, 128), BF16),
            vm((512, 128), BF16),
            vm((512, 2048), F32),
            vm((512, 2048), F32),
            vm((512, 1024), F32),
            vm((512, 1024), F32),
            vm((128, 2048), F32),
            vm((8, 2048), F32),
            vm((8, 2048), F32),
            vm((8, 2048), F32),
            vm((128, 1024), F32),
            vm((8, 1024), F32),
            vm((8, 1024), F32),
            vm((8, 1024), F32),
            pltpu.SemaphoreType.DMA((10,)),
            pltpu.SemaphoreType.DMA((2,)),
            pltpu.SemaphoreType.DMA((96,)),
            pltpu.SemaphoreType.DMA((16,)),
            pltpu.SemaphoreType.DMA((16,)),
            pltpu.SemaphoreType.DMA((16,)),
            pltpu.SemaphoreType.DMA((16,)),
            pltpu.SemaphoreType.DMA((9,)),
            pltpu.SemaphoreType.DMA((8,)),
            pltpu.SemaphoreType.DMA((16,)),
            pltpu.SemaphoreType.DMA((16,)),
            pltpu.SemaphoreType.DMA((8,)),
            pltpu.SemaphoreType.DMA((3,)),
        ],
        compiler_params=pltpu.CompilerParams(
            collective_id=0, has_side_effects=True, vmem_limit_bytes=56 * 1024 * 1024
        ),
        name="attention",
    )(
        pre_query[0],
        history_key[0],
        history_value[0],
        document_key[0],
        document_value[0],
        stretch_start,
        dec_q,
        cached_row_keys.reshape(32, 256, HEAD),
        cached_row_values.reshape(32, 256, HEAD),
        cache_lengths,
        doc_owner,
        new_key,
        new_value,
    )
    return pre[None], dec.reshape(32, 4, 512)


def solution(mesh):
    placed = (
        P("grp", "seq", "rep"),
        P("grp", "seq", "rep"),
        P("grp", "seq", "rep"),
        P("grp", "seq", "rep"),
        P("grp", "seq", "rep"),
        P("grp"),
        P(("grp", "rep"), None, "seq"),
        P(("grp", "rep"), "seq", None, None),
        P(("grp", "rep"), "seq", None, None),
        P(("grp", "rep")),
        P(("grp", "rep")),
        P(("grp", "rep"), None, None),
        P(("grp", "rep"), None, None),
    )
    return jax.shard_map(
        local,
        mesh=mesh,
        in_specs=placed,
        out_specs=(P("grp", "seq", "rep"), P(("grp", "rep"), None, "seq")),
        check_vma=False,
    )
```

```python
import functools

import jax
import jax.numpy as jnp
from jax import lax
from jax.experimental import pallas as pl
from jax.experimental.pallas import tpu as pltpu
from jax.sharding import PartitionSpec as P

HEAD = 128
LOG2E = 1.4426950408889634
SCALE = HEAD ** (-0.5) * LOG2E
LOW = -1e30
F32 = jnp.float32
BF16 = jnp.bfloat16
MESH = pl.DeviceIdType.MESH
NT = (((1,), (1,)), ((), ()))
NN = (((1,), (0,)), ((), ()))


def kernel(
    pre_query,
    hist_key,
    hist_value,
    doc_key,
    doc_value,
    start_ref,
    dec_query,
    cache_key,
    cache_value,
    length_ref,
    owner_ref,
    new_key,
    new_value,
    pre_out,
    dec_out,
    buf,
    vals,
    pre_q,
    pre_raw,
    pre_o,
    q_own,
    q_sib,
    ck,
    cv,
    kn,
    vn,
    o_own,
    l_own,
    o_snd,
    l_snd,
    o_sib,
    l_sib,
    dq,
    od_snd,
    od,
    oc,
    of,
    lt,
    qa,
    dec_o,
    s1,
    s2,
    d1,
    d2,
    acc,
    tot,
    mrun,
    macc,
    dacc,
    dtot,
    dmrun,
    dmacc,
    in_sem,
    out_sem,
    send_sem,
    r0,
    r1,
    r2,
    r3,
    rx,
    ra,
    rq,
    ro,
    rf,
    own_sem,
    pass_sem,
):
    grp = lax.axis_index("grp")
    seq = lax.axis_index("seq")
    rep = lax.axis_index("rep")
    y, xh, core = seq // 4, (seq // 2) % 2, seq % 2
    run = core
    chip = seq // 2

    def seq_at(dy, other):
        return ((y + dy) % 4) * 4 + (xh + other) % 2 * 2 + core

    up = {"seq": seq_at(1, 0)}
    down = {"seq": seq_at(3, 0)}
    across = {"seq": seq_at(0, 1)}
    sib = {"seq": seq + 1 - 2 * core}
    own_slot = grp * 8 + rep
    plane = [((chip + k) % 8, {"seq": (chip + k) % 8 * 2 + core}) for k in range(8)]
    column = []
    for k in range(16):
        slot = (own_slot + k) % 16
        column.append((slot, {"grp": slot // 8, "rep": slot % 8}))

    own_head = pl.ds(pl.multiple_of(chip * 128, 128), 128)
    loads = [
        pltpu.make_async_copy(hist_key, buf.at[seq, pl.ds(512, 128)], in_sem.at[0]),
        pltpu.make_async_copy(doc_key, buf.at[seq, pl.ds(0, 256)], in_sem.at[1]),
        pltpu.make_async_copy(hist_value, vals.at[pl.ds(0, 128)], in_sem.at[2]),
        pltpu.make_async_copy(doc_value, vals.at[pl.ds(128, 256)], in_sem.at[3]),
        pltpu.make_async_copy(dec_query, q_own, in_sem.at[4]),
        pltpu.make_async_copy(cache_key, ck, in_sem.at[5]),
        pltpu.make_async_copy(cache_value, cv, in_sem.at[6]),
        pltpu.make_async_copy(pre_query, pre_raw, in_sem.at[7]),
        pltpu.make_async_copy(new_key.at[:, :, own_head], kn, in_sem.at[8]),
        pltpu.make_async_copy(new_value.at[:, :, own_head], vn, in_sem.at[9]),
    ]
    for c in loads:
        c.start()

    barrier = pltpu.get_barrier_semaphore()
    partners = [sib] + [p[1] for p in plane[1:]] + [p[1] for p in column[1:]]
    for d in partners:
        pl.semaphore_signal(barrier, inc=1, device_id=d, device_id_type=MESH)

    for c in loads[:4]:
        c.wait()
    for i, at in ((0, 640), (1, 256), (2, 384)):
        v = vals[i * 128 : (i + 1) * 128, :]
        buf[seq, at : at + 128, :] = v.astype(F32).T.astype(BF16)
    loads[4].wait()
    q_own[...] = (q_own[...].astype(F32) * SCALE).astype(BF16)
    pl.semaphore_wait(barrier, len(partners))

    sends = []

    def send(src, dst, recv, dev):
        c = pltpu.make_async_remote_copy(
            src_ref=src,
            dst_ref=dst,
            send_sem=send_sem.at[len(sends)],
            recv_sem=recv,
            device_id=dev,
            device_id_type=MESH,
        )
        c.start()
        sends.append(c)

    def arrived(dst, recv):
        pltpu.make_async_remote_copy(
            src_ref=dst,
            dst_ref=dst,
            send_sem=send_sem.at[0],
            recv_sem=recv,
            device_id=sib,
            device_id_type=MESH,
        ).wait_recv()

    class Part:
        def __init__(self, at, size, sem_a, sem_b):
            self.whole = pl.ds(at, size)
            self.first = pl.ds(at, size // 2)
            self.second = pl.ds(at + size // 2, size // 2)
            self.sem_a, self.sem_b = sem_a, sem_b

        def send(self, b, *devs):
            for dev in devs:
                ref = buf.at[b, self.whole]
                send(ref, ref, self.sem_a.at[b], dev)

        def send_first(self, b, *devs):
            for dev in devs:
                ref = buf.at[b, self.first]
                send(ref, ref, self.sem_a.at[b], dev)

        def send_second(self, b, *devs):
            for dev in devs:
                ref = buf.at[b, self.second]
                send(ref, ref, self.sem_b.at[b], dev)

        def wait(self, b):
            arrived(buf.at[b, self.whole], self.sem_a.at[b])

        def wait_first(self, b):
            arrived(buf.at[b, self.first], self.sem_a.at[b])

        def wait_second(self, b):
            arrived(buf.at[b, self.second], self.sem_b.at[b])

        def wait_sib(self, row):
            for x in range(2):
                self.wait(row * 4 + x * 2 + 1 - core)

    doc = Part(0, 512, r0, r1)
    hist = Part(512, 256, r2, r3)
    far, below, above = seq_at(0, 1), seq_at(3, 0), seq_at(1, 0)
    far_below, far_above = seq_at(3, 1), seq_at(1, 1)

    send(q_own, q_sib, rx.at[0], sib)
    doc.send_first(seq, across)
    doc.send_second(seq, across)
    doc.send(seq, up, down, sib)

    def piece(ref, i):
        return ref.at[pl.ds(pl.multiple_of(i * 64, 64), 64)]

    own_copies = [
        pltpu.make_async_copy(piece(q_own, chip), qa.at[chip], own_sem.at[0]),
        pltpu.make_async_copy(qa.at[rep], piece(dq, own_slot), own_sem.at[1]),
        pltpu.make_async_copy(od_snd.at[own_slot], od.at[own_slot], own_sem.at[2]),
    ]
    own_copies[0].start()
    for j, dev in plane[1:]:
        send(piece(q_own, j), qa.at[chip], ra.at[chip], dev)

    def cache_rows(group):
        for i in range(8):
            r = group * 8 + i
            rows = pl.ds(r * 16, 16)
            q = jnp.concatenate([q_own[rows, :], q_sib[rows, :]], axis=0)
            s = lax.dot_general(q, ck[r], NT, preferred_element_type=F32)
            at = run * 256 + lax.broadcasted_iota(jnp.int32, (32, 256), 1)
            seen = at < length_ref[r]
            s = jnp.where(seen, s, LOW)
            m = jnp.max(s, axis=1, keepdims=True)
            p = jnp.where(seen, jnp.exp2(s - m), 0.0)
            l = jnp.sum(p, axis=1, keepdims=True)
            o = lax.dot_general(p.astype(BF16), cv[r], NN, preferred_element_type=F32)
            safe = jnp.maximum(l, 1e-30)
            o = o / safe
            top = jnp.where(l > 0.0, m + jnp.log(safe) * LOG2E, LOW)
            top = jnp.broadcast_to(top, (32, 128))
            o_own[rows, :] = o[:16]
            l_own[rows, :] = top[:16]
            o_snd[rows, :] = o[16:].astype(BF16)
            l_snd[rows, :] = top[16:]

    arrived(q_sib, rx.at[0])
    loads[5].wait()
    loads[6].wait()
    cache_rows(0)

    doc.wait_first(far)
    doc.send_first(far, up, down)
    doc.wait(below)
    doc.send_first(below, up)
    doc.send(below, sib)
    doc.wait(above)
    doc.send_second(above, down)
    doc.send(above, sib)
    cache_rows(1)
    doc.wait_second(far)
    doc.send_second(far, up, down)
    doc.send(far, sib)
    hist.send_first(seq, across)
    hist.send_second(seq, across)
    hist.send(seq, up, down, sib)

    own_copies[0].wait()
    for j, _ in plane[1:]:
        arrived(qa.at[j], ra.at[j])
    own_copies[1].start()
    for slot, dev in column[1:]:
        send(qa.at[slot % 8], piece(dq, own_slot), rq.at[own_slot], dev)
    cache_rows(2)
    doc.wait_first(far_below)
    doc.send_first(far_below, up)
    doc.wait_second(far_above)
    doc.send_second(far_above, down)
    cache_rows(3)
    send(o_snd, o_sib, rx.at[3], sib)
    send(l_snd, l_sib, rx.at[4], sib)

    doc.wait_second(far_below)
    doc.send(far_below, sib)
    doc.wait_first(far_above)
    doc.send(far_above, sib)
    hist.wait_first(far)
    hist.send_first(far, up, down)
    hist.wait(below)
    hist.send_first(below, up)
    hist.send(below, sib)
    hist.wait(above)
    hist.send_second(above, down)
    hist.send(above, sib)
    hist.wait_second(far)
    hist.send_second(far, up, down)
    hist.send(far, sib)

    loads[7].wait()
    for h in range(8):
        x = pre_raw[:, h * 128 : (h + 1) * 128].astype(F32) * SCALE
        pre_q[h * 256 : (h + 1) * 256, :] = x.astype(BF16)

    acc[...] = jnp.zeros_like(acc)
    tot[...] = jnp.zeros_like(tot)
    mrun[...] = jnp.full_like(mrun, LOW)
    macc[...] = jnp.full_like(macc, LOW)

    def hist_keys(row):
        return jnp.concatenate([buf[row * 4 + c, 512:640, :] for c in range(4)], axis=0)

    def hist_vals(row):
        return jnp.concatenate([buf[row * 4 + c, 640:768, :] for c in range(4)], axis=1)

    def doc_keys(c):
        return jnp.concatenate([buf[c * 2 + i, 0:256, :] for i in range(2)], axis=0)

    def doc_vals(c):
        parts = [buf[c * 2 + i, 256 + 128 * j : 384 + 128 * j, :] for i in range(2) for j in range(2)]
        return jnp.concatenate(parts, axis=1)

    def score(q, keys, out, top, mask=None):
        lanes = q.shape[0]
        s = lax.dot_general(keys, q[...], NT, preferred_element_type=F32)
        if mask is not None:
            s = mask(s)
        out[:, :lanes] = s
        return jnp.maximum(top, jnp.max(s.reshape(64, 8, lanes), axis=0))

    def weigh(s, vals_t, m, state):
        a, t, ma = state
        lanes = a.shape[1]
        now = jnp.max(m, axis=0, keepdims=True)
        before = jnp.max(ma[...], axis=0, keepdims=True)
        f = jnp.exp2(before - now)
        p = jnp.exp2(s[:, :lanes] - now)
        t[...] = t[...] * f + jnp.sum(p.reshape(64, 8, lanes), axis=0)
        a[...] = a[...] * f + lax.dot_general(
            vals_t, p.astype(BF16), NN, preferred_element_type=F32
        )
        ma[...] = m

    pre_state = (acc, tot, macc)

    def hist_mask(row):
        def mask(s):
            slot = row * 512 + lax.broadcasted_iota(jnp.int32, (512, 128), 0)
            bias = jnp.where(slot < start_ref[0], 0.0, LOW)
            return s + jnp.concatenate([bias] * 16, axis=1)

        return mask

    def causal_mask(s):
        key_at = lax.broadcasted_iota(jnp.int32, s.shape, 0)
        query_at = core * 256 + (lax.broadcasted_iota(jnp.int32, s.shape, 1) & 255)
        return jnp.where(key_at <= query_at, s, LOW)

    def step(keys, out, mask, s, vals_t):
        m = mrun[...]
        new = score(pre_q, keys, out, m, mask)
        weigh(s, vals_t, m, pre_state)
        mrun[...] = new

    doc.wait_sib(y)

    @pl.when(xh == 1)
    def _():
        mrun[...] = score(pre_q, doc_keys(chip), s1, mrun[...], causal_mask)
        step(doc_keys(y * 2), s2, None, s1, doc_vals(chip))

    @pl.when(xh == 0)
    def _():
        mrun[...] = score(pre_q, doc_keys(chip), s2, mrun[...], causal_mask)

    def row_of(k):
        return (y + jnp.where(k == 0, 0, jnp.where(k == 1, 3, k - 1))) % 4

    own_copies[1].wait()
    for slot, _ in column[1:]:
        arrived(piece(dq, slot), rq.at[slot])
    dec_state = (dacc, dtot, dmacc)
    dacc[...] = jnp.zeros_like(dacc)
    dtot[...] = jnp.zeros_like(dtot)
    dmacc[...] = jnp.full_like(dmacc, LOW)

    def dec_step(keys, out, s, vals_t):
        m = dmrun[...]
        new = score(dq, keys, out, m)
        weigh(s, vals_t, m, dec_state)
        dmrun[...] = new

    def dec_row(k, _):
        row = row_of(k)
        doc.wait_sib(row)
        dec_step(doc_keys(row * 2), d1, d2, doc_vals(row_of(k - 1) * 2 + 1))
        dec_step(doc_keys(row * 2 + 1), d2, d1, doc_vals(row * 2))
        return 0

    dmrun[...] = score(dq, doc_keys(y * 2), d1, jnp.full(dmrun.shape, LOW, F32))
    dec_step(doc_keys(y * 2 + 1), d2, d1, doc_vals(y * 2))
    dec_row(1, 0)
    for x in range(2):
        b = seq_at(2, x)
        doc.wait_first(b)
        doc.wait_second(b)
        doc.send(b, sib)
    dec_row(2, 0)
    dec_row(3, 0)
    row = (y + 2) % 4
    weigh(d2, doc_vals(row * 2 + 1), dmrun[...], dec_state)
    total = jnp.sum(dtot[...], axis=0, keepdims=True)
    level = jnp.max(dmacc[...], axis=0, keepdims=True) + jnp.log(total) * LOG2E
    od_snd[:, 0:64, :] = (dacc[...] / total).T.astype(BF16).reshape(16, 64, 128)
    line = lax.broadcasted_iota(jnp.int32, (16, 128), 0)
    for k in range(8):
        whole = level[:, k * 128 : (k + 1) * 128]
        high = whole.astype(BF16).astype(F32)
        mid = (whole - high).astype(BF16).astype(F32)
        low = whole - high - mid
        three = jnp.where(line == 0, high, jnp.where(line == 1, mid, jnp.where(line == 2, low, 0.0)))
        for i in range(2):
            od_snd[2 * k + i, 64:80, :] = three.astype(BF16)
    own_copies[2].start()
    for slot, dev in column[1:]:
        send(od_snd.at[slot], od.at[own_slot], ro.at[own_slot], dev)

    def row_step(k, waiting):
        row = row_of(k)

        @pl.when(row < y)
        def _():
            step(doc_keys(row * 2), s1, None, s2, doc_vals(waiting))
            step(doc_keys(row * 2 + 1), s2, None, s1, doc_vals(row * 2))

        return jnp.where(row < y, row * 2 + 1, waiting)

    hist.wait_first(far_below)
    hist.send_first(far_below, up)
    hist.wait_second(far_above)
    hist.send_second(far_above, down)
    hist.wait_second(far_below)
    hist.send(far_below, sib)
    hist.wait_first(far_above)
    hist.send(far_above, sib)
    waiting = lax.fori_loop(1, 3, row_step, y * 2)
    for x in range(2):
        b = seq_at(2, x)
        hist.wait_first(b)
        hist.wait_second(b)
        hist.send(b, sib)

    def hist_pair(a, b, vals_t):
        hist.wait_sib(a)
        hist.wait_sib(b)
        step(hist_keys(a), s1, hist_mask(a), s2, vals_t)
        step(hist_keys(b), s2, hist_mask(b), s1, hist_vals(a))


    owners = [owner_ref[chip * 4 + i] for i in range(4)]
    rows_owner = jnp.concatenate([jnp.full((16, 128), o, jnp.int32) for o in owners], axis=0)
    lane = (lax.broadcasted_iota(jnp.int32, (16, 128), 1) >> 4) & 3
    lane_owner = jnp.where(
        lane == 0, owners[0], jnp.where(lane == 1, owners[1], jnp.where(lane == 2, owners[2], owners[3]))
    )
    which = jnp.concatenate([rows_owner, lane_owner], axis=0) == 0
    own_copies[2].wait()
    passed = []
    for k in (0, 1, 7, 2, 6, 3, 5, 4):
        h = (rep + k) % 8
        for g in range(2):
            slot = (grp + g) % 2 * 8 + h
            if k + g > 0:
                arrived(od.at[slot], ro.at[slot])
        chosen = jnp.where(which, od[h].astype(F32), od[8 + h].astype(F32))
        oc[h] = chosen.astype(BF16)
        copy = pltpu.make_async_remote_copy(
            src_ref=oc.at[h],
            dst_ref=of.at[chip],
            send_sem=pass_sem.at[k],
            recv_sem=rf.at[chip],
            device_id={"seq": h * 2 + core},
            device_id_type=MESH,
        )
        passed.append((h, copy))

        @pl.when(h != chip)
        def _(copy=copy):
            copy.start()

    of[chip] = oc[chip]

    waiting = row_step(3, waiting)
    hist_pair(y, (y + 3) % 4, doc_vals(waiting))
    hist_pair((y + 1) % 4, row, hist_vals((y + 3) % 4))
    weigh(s2, hist_vals(row), mrun[...], pre_state)
    total = jnp.sum(tot[...], axis=0, keepdims=True)
    for h in range(8):
        cols = slice(h * 256, (h + 1) * 256)
        o = acc[:, cols] / total[:, cols]
        pre_o[:, h * 128 : (h + 1) * 128] = o.T.astype(BF16)
    pre_copy = pltpu.make_async_copy(pre_o, pre_out, out_sem.at[0])
    pre_copy.start()

    loads[8].wait()
    loads[9].wait()
    new_k = kn[...].astype(F32).reshape(128, 128).astype(BF16)
    new_v = vn[...].astype(F32).reshape(128, 128).astype(BF16)
    arrived(o_sib, rx.at[3])
    arrived(l_sib, rx.at[4])
    for j, _ in plane[1:]:
        arrived(of.at[j], rf.at[j])
    sums = [jnp.sum(of[j, 64:80, :].astype(F32), axis=0, keepdims=True) for j in range(8)]
    lt[...] = jnp.concatenate(sums * 16, axis=0).T
    levels = lt[pl.ds(pl.multiple_of(rep % 2 * 64, 64), 64), :]
    for c in range(4):
        rows = slice(c * 128, (c + 1) * 128)
        l_doc = jnp.concatenate(
            [jnp.broadcast_to(levels[:, j : j + 1], (64, 128)) for j in (2 * c, 2 * c + 1)], axis=0
        )
        o_doc = jnp.concatenate([of[j, 0:64, :].astype(F32) for j in (2 * c, 2 * c + 1)], axis=0)
        s = lax.dot_general(q_own[rows, :], new_k, NT, preferred_element_type=F32)
        line = c * 128 + lax.broadcasted_iota(jnp.int32, (128, 128), 0)
        col = lax.broadcasted_iota(jnp.int32, (128, 128), 1)
        seen = ((line >> 4) == (col >> 2)) & ((col & 3) <= ((line >> 2) & 3))
        s = jnp.where(seen, s, LOW)
        m = jnp.max(s, axis=1, keepdims=True)
        top = jnp.maximum(jnp.maximum(l_doc, l_own[rows, :]), jnp.maximum(l_sib[rows, :], m))
        p = jnp.where(seen, jnp.exp2(s - top), 0.0)
        w_doc = jnp.exp2(l_doc - top)
        w_own = jnp.exp2(l_own[rows, :] - top)
        w_sib = jnp.exp2(l_sib[rows, :] - top)
        o = lax.dot_general(p.astype(BF16), new_v, NN, preferred_element_type=F32)
        o = o + w_doc * o_doc + w_own * o_own[rows, :] + w_sib * o_sib[rows, :].astype(F32)
        weight = jnp.sum(p, axis=1, keepdims=True) + w_doc + w_own + w_sib
        dec_o[rows, :] = (o / weight).astype(BF16)
    dec_copy = pltpu.make_async_copy(dec_o, dec_out, out_sem.at[1])
    dec_copy.start()
    for c in sends:
        c.wait_send()
    for h, copy in passed:

        @pl.when(h != chip)
        def _(copy=copy):
            copy.wait_send()

    pre_copy.wait()
    dec_copy.wait()


def local(
    pre_query,
    history_key,
    history_value,
    document_key,
    document_value,
    stretch_start,
    decode_query,
    cached_row_keys,
    cached_row_values,
    cache_lengths,
    doc_owner,
    decode_key,
    decode_value,
):
    dec_q = decode_query.reshape(512, HEAD)
    smem = pl.BlockSpec(memory_space=pltpu.SMEM)
    hbm = pl.BlockSpec(memory_space=pl.ANY)

    def vm(shape, dtype):
        return pltpu.VMEM(shape, dtype)

    pre, dec = pl.pallas_call(
        kernel,
        out_shape=(
            jax.ShapeDtypeStruct((256, 1024), BF16),
            jax.ShapeDtypeStruct((512, 128), BF16),
        ),
        in_specs=[hbm, hbm, hbm, hbm, hbm, smem, hbm, hbm, hbm, smem, smem, hbm, hbm],
        out_specs=(hbm, hbm),
        scratch_shapes=[
            vm((16, 768, 128), BF16),
            vm((384, 128), BF16),
            vm((2048, 128), BF16),
            vm((256, 1024), BF16),
            vm((256, 1024), BF16),
            vm((512, 128), BF16),
            vm((512, 128), BF16),
            vm((32, 256, 128), BF16),
            vm((32, 256, 128), BF16),
            vm((32, 4, 128), BF16),
            vm((32, 4, 128), BF16),
            vm((512, 128), F32),
            vm((512, 128), F32),
            vm((512, 128), BF16),
            vm((512, 128), F32),
            vm((512, 128), BF16),
            vm((512, 128), F32),
            vm((1024, 128), BF16),
            vm((16, 80, 128), BF16),
            vm((16, 80, 128), BF16),
            vm((8, 80, 128), BF16),
            vm((8, 80, 128), BF16),
            vm((128, 128), F32),
            vm((8, 64, 128), BF16),
            vm((512, 128), BF16),
            vm((512, 2048), F32),
            vm((512, 2048), F32),
            vm((512, 1024), F32),
            vm((512, 1024), F32),
            vm((128, 2048), F32),
            vm((8, 2048), F32),
            vm((8, 2048), F32),
            vm((8, 2048), F32),
            vm((128, 1024), F32),
            vm((8, 1024), F32),
            vm((8, 1024), F32),
            vm((8, 1024), F32),
            pltpu.SemaphoreType.DMA((10,)),
            pltpu.SemaphoreType.DMA((2,)),
            pltpu.SemaphoreType.DMA((96,)),
            pltpu.SemaphoreType.DMA((16,)),
            pltpu.SemaphoreType.DMA((16,)),
            pltpu.SemaphoreType.DMA((16,)),
            pltpu.SemaphoreType.DMA((16,)),
            pltpu.SemaphoreType.DMA((9,)),
            pltpu.SemaphoreType.DMA((8,)),
            pltpu.SemaphoreType.DMA((16,)),
            pltpu.SemaphoreType.DMA((16,)),
            pltpu.SemaphoreType.DMA((8,)),
            pltpu.SemaphoreType.DMA((3,)),
            pltpu.SemaphoreType.DMA((8,)),
        ],
        compiler_params=pltpu.CompilerParams(
            collective_id=0, has_side_effects=True, vmem_limit_bytes=56 * 1024 * 1024
        ),
        name="attention",
    )(
        pre_query[0],
        history_key[0],
        history_value[0],
        document_key[0],
        document_value[0],
        stretch_start,
        dec_q,
        cached_row_keys.reshape(32, 256, HEAD),
        cached_row_values.reshape(32, 256, HEAD),
        cache_lengths,
        doc_owner,
        decode_key,
        decode_value,
    )
    return pre[None], dec.reshape(32, 4, 512)


def solution(mesh):
    placed = (
        P("grp", "seq", "rep"),
        P("grp", "seq", "rep"),
        P("grp", "seq", "rep"),
        P("grp", "seq", "rep"),
        P("grp", "seq", "rep"),
        P("grp"),
        P(("grp", "rep"), None, "seq"),
        P(("grp", "rep"), "seq", None, None),
        P(("grp", "rep"), "seq", None, None),
        P(("grp", "rep")),
        P(("grp", "rep")),
        P(("grp", "rep"), None, None),
        P(("grp", "rep"), None, None),
    )
    return jax.shard_map(
        local,
        mesh=mesh,
        in_specs=placed,
        out_specs=(P("grp", "seq", "rep"), P(("grp", "rep"), None, "seq")),
        check_vma=False,
    )
```

```python
import functools

import jax
import jax.numpy as jnp
from jax import lax
from jax.experimental import pallas as pl
from jax.experimental.pallas import tpu as pltpu
from jax.sharding import PartitionSpec as P

HEAD = 128
LOG2E = 1.4426950408889634
SCALE = HEAD ** (-0.5) * LOG2E
LOW = -1e30
F32 = jnp.float32
BF16 = jnp.bfloat16
MESH = pl.DeviceIdType.MESH
NT = (((1,), (1,)), ((), ()))
NN = (((1,), (0,)), ((), ()))


def kernel(
    pre_query,
    hist_key,
    hist_value,
    doc_key,
    doc_value,
    start_ref,
    dec_query,
    cache_key,
    cache_value,
    length_ref,
    owner_ref,
    new_key,
    new_value,
    pre_out,
    dec_out,
    buf,
    vals,
    pre_q,
    pre_raw,
    pre_o,
    q_own,
    q_sib,
    ck,
    cv,
    kn,
    vn,
    o_own,
    l_own,
    o_snd,
    l_snd,
    o_sib,
    l_sib,
    dq,
    od_snd,
    od,
    oc,
    of,
    lt,
    qa,
    dec_o,
    s1,
    s2,
    d1,
    d2,
    acc,
    tot,
    mrun,
    macc,
    dacc,
    dtot,
    dmrun,
    dmacc,
    in_sem,
    out_sem,
    send_sem,
    r0,
    r1,
    r2,
    r3,
    rx,
    ra,
    rq,
    ro,
    rf,
    own_sem,
    pass_sem,
):
    grp = lax.axis_index("grp")
    seq = lax.axis_index("seq")
    rep = lax.axis_index("rep")
    y, xh, core = seq // 4, (seq // 2) % 2, seq % 2
    run = core
    chip = seq // 2

    def seq_at(dy, other):
        return ((y + dy) % 4) * 4 + (xh + other) % 2 * 2 + core

    up = {"seq": seq_at(1, 0)}
    down = {"seq": seq_at(3, 0)}
    across = {"seq": seq_at(0, 1)}
    sib = {"seq": seq + 1 - 2 * core}
    own_slot = grp * 8 + rep
    plane = [((chip + k) % 8, {"seq": (chip + k) % 8 * 2 + core}) for k in range(8)]
    column = []
    for k in range(16):
        slot = (own_slot + k) % 16
        column.append((slot, {"grp": slot // 8, "rep": slot % 8}))

    own_head = pl.ds(pl.multiple_of(chip * 128, 128), 128)
    loads = [
        pltpu.make_async_copy(hist_key, buf.at[seq, pl.ds(512, 128)], in_sem.at[0]),
        pltpu.make_async_copy(doc_key, buf.at[seq, pl.ds(0, 256)], in_sem.at[1]),
        pltpu.make_async_copy(hist_value, vals.at[pl.ds(0, 128)], in_sem.at[2]),
        pltpu.make_async_copy(doc_value, vals.at[pl.ds(128, 256)], in_sem.at[3]),
        pltpu.make_async_copy(dec_query, q_own, in_sem.at[4]),
        pltpu.make_async_copy(cache_key, ck, in_sem.at[5]),
        pltpu.make_async_copy(cache_value, cv, in_sem.at[6]),
        pltpu.make_async_copy(pre_query, pre_raw, in_sem.at[7]),
        pltpu.make_async_copy(new_key.at[:, :, own_head], kn, in_sem.at[8]),
        pltpu.make_async_copy(new_value.at[:, :, own_head], vn, in_sem.at[9]),
    ]
    for c in loads:
        c.start()

    barrier = pltpu.get_barrier_semaphore()
    partners = [sib] + [p[1] for p in plane[1:]] + [p[1] for p in column[1:]]
    for d in partners:
        pl.semaphore_signal(barrier, inc=1, device_id=d, device_id_type=MESH)

    for c in loads[:4]:
        c.wait()
    for i, at in ((0, 640), (1, 256), (2, 384)):
        v = vals[i * 128 : (i + 1) * 128, :]
        buf[seq, at : at + 128, :] = v.astype(F32).T.astype(BF16)
    loads[4].wait()
    q_own[...] = (q_own[...].astype(F32) * SCALE).astype(BF16)
    pl.semaphore_wait(barrier, len(partners))

    sends = []

    def send(src, dst, recv, dev):
        c = pltpu.make_async_remote_copy(
            src_ref=src,
            dst_ref=dst,
            send_sem=send_sem.at[len(sends)],
            recv_sem=recv,
            device_id=dev,
            device_id_type=MESH,
        )
        c.start()
        sends.append(c)

    def arrived(dst, recv):
        pltpu.make_async_remote_copy(
            src_ref=dst,
            dst_ref=dst,
            send_sem=send_sem.at[0],
            recv_sem=recv,
            device_id=sib,
            device_id_type=MESH,
        ).wait_recv()

    class Part:
        def __init__(self, at, size, sem_a, sem_b):
            self.whole = pl.ds(at, size)
            self.first = pl.ds(at, size // 2)
            self.second = pl.ds(at + size // 2, size // 2)
            self.sem_a, self.sem_b = sem_a, sem_b

        def send(self, b, *devs):
            for dev in devs:
                ref = buf.at[b, self.whole]
                send(ref, ref, self.sem_a.at[b], dev)

        def send_first(self, b, *devs):
            for dev in devs:
                ref = buf.at[b, self.first]
                send(ref, ref, self.sem_a.at[b], dev)

        def send_second(self, b, *devs):
            for dev in devs:
                ref = buf.at[b, self.second]
                send(ref, ref, self.sem_b.at[b], dev)

        def wait(self, b):
            arrived(buf.at[b, self.whole], self.sem_a.at[b])

        def wait_first(self, b):
            arrived(buf.at[b, self.first], self.sem_a.at[b])

        def wait_second(self, b):
            arrived(buf.at[b, self.second], self.sem_b.at[b])

        def wait_sib(self, row):
            for x in range(2):
                self.wait(row * 4 + x * 2 + 1 - core)

    doc = Part(0, 512, r0, r1)
    hist = Part(512, 256, r2, r3)
    far, below, above = seq_at(0, 1), seq_at(3, 0), seq_at(1, 0)
    far_below, far_above = seq_at(3, 1), seq_at(1, 1)

    send(q_own, q_sib, rx.at[0], sib)
    doc.send_first(seq, across)
    doc.send_second(seq, across)
    doc.send(seq, up, down, sib)

    def piece(ref, i):
        return ref.at[pl.ds(pl.multiple_of(i * 64, 64), 64)]

    own_copies = [
        pltpu.make_async_copy(piece(q_own, chip), qa.at[chip], own_sem.at[0]),
        pltpu.make_async_copy(qa.at[rep], piece(dq, own_slot), own_sem.at[1]),
        pltpu.make_async_copy(od_snd.at[own_slot], od.at[own_slot], own_sem.at[2]),
    ]

    def cache_rows(group):
        for i in range(8):
            r = group * 8 + i
            rows = pl.ds(r * 16, 16)
            q = jnp.concatenate([q_own[rows, :], q_sib[rows, :]], axis=0)
            s = lax.dot_general(q, ck[r], NT, preferred_element_type=F32)
            at = run * 256 + lax.broadcasted_iota(jnp.int32, (32, 256), 1)
            seen = at < length_ref[r]
            s = jnp.where(seen, s, LOW)
            m = jnp.max(s, axis=1, keepdims=True)
            p = jnp.where(seen, jnp.exp2(s - m), 0.0)
            l = jnp.sum(p, axis=1, keepdims=True)
            o = lax.dot_general(p.astype(BF16), cv[r], NN, preferred_element_type=F32)
            safe = jnp.maximum(l, 1e-30)
            o = o / safe
            top = jnp.where(l > 0.0, m + jnp.log(safe) * LOG2E, LOW)
            top = jnp.broadcast_to(top, (32, 128))
            o_own[rows, :] = o[:16]
            l_own[rows, :] = top[:16]
            o_snd[rows, :] = o[16:].astype(BF16)
            l_snd[rows, :] = top[16:]

    arrived(q_sib, rx.at[0])
    loads[5].wait()
    loads[6].wait()
    cache_rows(0)

    doc.wait_first(far)
    doc.send_first(far, up, down)
    doc.wait(below)
    doc.send_first(below, up)
    doc.send(below, sib)
    doc.wait(above)
    doc.send_second(above, down)
    doc.send(above, sib)
    own_copies[0].start()
    for j, dev in plane[1:]:
        send(piece(q_own, j), qa.at[chip], ra.at[chip], dev)
    cache_rows(1)
    doc.wait_second(far)
    doc.send_second(far, up, down)
    doc.send(far, sib)
    hist.send_first(seq, across)
    hist.send_second(seq, across)
    hist.send(seq, up, down, sib)

    cache_rows(2)
    doc.wait_first(far_below)
    doc.send_first(far_below, up)
    doc.wait_second(far_above)
    doc.send_second(far_above, down)
    own_copies[0].wait()
    for j, _ in plane[1:]:
        arrived(qa.at[j], ra.at[j])
    own_copies[1].start()
    for slot, dev in column[1:]:
        send(qa.at[slot % 8], piece(dq, own_slot), rq.at[own_slot], dev)
    cache_rows(3)
    send(o_snd, o_sib, rx.at[3], sib)
    send(l_snd, l_sib, rx.at[4], sib)

    doc.wait_second(far_below)
    doc.send(far_below, sib)
    doc.wait_first(far_above)
    doc.send(far_above, sib)

    loads[7].wait()
    for h in range(8):
        x = pre_raw[:, h * 128 : (h + 1) * 128].astype(F32) * SCALE
        pre_q[h * 256 : (h + 1) * 256, :] = x.astype(BF16)

    acc[...] = jnp.zeros_like(acc)
    tot[...] = jnp.zeros_like(tot)
    mrun[...] = jnp.full_like(mrun, LOW)
    macc[...] = jnp.full_like(macc, LOW)

    def hist_keys(row):
        return jnp.concatenate([buf[row * 4 + c, 512:640, :] for c in range(4)], axis=0)

    def hist_vals(row):
        return jnp.concatenate([buf[row * 4 + c, 640:768, :] for c in range(4)], axis=1)

    def doc_keys(c):
        return jnp.concatenate([buf[c * 2 + i, 0:256, :] for i in range(2)], axis=0)

    def doc_vals(c):
        parts = [buf[c * 2 + i, 256 + 128 * j : 384 + 128 * j, :] for i in range(2) for j in range(2)]
        return jnp.concatenate(parts, axis=1)

    def score(q, keys, out, top, mask=None):
        lanes = q.shape[0]
        s = lax.dot_general(keys, q[...], NT, preferred_element_type=F32)
        if mask is not None:
            s = mask(s)
        out[:, :lanes] = s
        return jnp.maximum(top, jnp.max(s.reshape(64, 8, lanes), axis=0))

    def weigh(s, vals_t, m, state):
        a, t, ma = state
        lanes = a.shape[1]
        now = jnp.max(m, axis=0, keepdims=True)
        before = jnp.max(ma[...], axis=0, keepdims=True)
        f = jnp.exp2(before - now)
        p = jnp.exp2(s[:, :lanes] - now)
        t[...] = t[...] * f + jnp.sum(p.reshape(64, 8, lanes), axis=0)
        a[...] = a[...] * f + lax.dot_general(
            vals_t, p.astype(BF16), NN, preferred_element_type=F32
        )
        ma[...] = m

    pre_state = (acc, tot, macc)

    def hist_mask(row):
        def mask(s):
            slot = row * 512 + lax.broadcasted_iota(jnp.int32, (512, 128), 0)
            bias = jnp.where(slot < start_ref[0], 0.0, LOW)
            return s + jnp.concatenate([bias] * 16, axis=1)

        return mask

    def causal_mask(s):
        key_at = lax.broadcasted_iota(jnp.int32, s.shape, 0)
        query_at = core * 256 + (lax.broadcasted_iota(jnp.int32, s.shape, 1) & 255)
        return jnp.where(key_at <= query_at, s, LOW)

    def step(keys, out, mask, s, vals_t):
        m = mrun[...]
        new = score(pre_q, keys, out, m, mask)
        weigh(s, vals_t, m, pre_state)
        mrun[...] = new

    doc.wait_sib(y)

    @pl.when(xh == 1)
    def _():
        mrun[...] = score(pre_q, doc_keys(chip), s1, mrun[...], causal_mask)
        step(doc_keys(y * 2), s2, None, s1, doc_vals(chip))

    @pl.when(xh == 0)
    def _():
        mrun[...] = score(pre_q, doc_keys(chip), s2, mrun[...], causal_mask)

    def row_of(k):
        return (y + jnp.where(k == 0, 0, jnp.where(k == 1, 3, k - 1))) % 4

    own_copies[1].wait()
    for slot, _ in column[1:]:
        arrived(piece(dq, slot), rq.at[slot])
    dec_state = (dacc, dtot, dmacc)
    dacc[...] = jnp.zeros_like(dacc)
    dtot[...] = jnp.zeros_like(dtot)
    dmacc[...] = jnp.full_like(dmacc, LOW)

    def dec_step(keys, out, s, vals_t):
        m = dmrun[...]
        new = score(dq, keys, out, m)
        weigh(s, vals_t, m, dec_state)
        dmrun[...] = new

    def dec_row(k, _):
        row = row_of(k)
        doc.wait_sib(row)
        dec_step(doc_keys(row * 2), d1, d2, doc_vals(row_of(k - 1) * 2 + 1))
        dec_step(doc_keys(row * 2 + 1), d2, d1, doc_vals(row * 2))
        return 0

    dmrun[...] = score(dq, doc_keys(y * 2), d1, jnp.full(dmrun.shape, LOW, F32))
    dec_step(doc_keys(y * 2 + 1), d2, d1, doc_vals(y * 2))
    dec_row(1, 0)
    for x in range(2):
        b = seq_at(2, x)
        doc.wait_first(b)
        doc.wait_second(b)
        doc.send(b, sib)
    hist.wait_first(far)
    hist.send_first(far, up, down)
    hist.wait(below)
    hist.send_first(below, up)
    hist.send(below, sib)
    hist.wait(above)
    hist.send_second(above, down)
    hist.send(above, sib)
    hist.wait_second(far)
    hist.send_second(far, up, down)
    hist.send(far, sib)
    dec_row(2, 0)
    dec_row(3, 0)
    row = (y + 2) % 4
    weigh(d2, doc_vals(row * 2 + 1), dmrun[...], dec_state)
    total = jnp.sum(dtot[...], axis=0, keepdims=True)
    level = jnp.max(dmacc[...], axis=0, keepdims=True) + jnp.log(total) * LOG2E
    od_snd[:, 0:64, :] = (dacc[...] / total).T.astype(BF16).reshape(16, 64, 128)
    line = lax.broadcasted_iota(jnp.int32, (16, 128), 0)
    for k in range(8):
        whole = level[:, k * 128 : (k + 1) * 128]
        high = whole.astype(BF16).astype(F32)
        mid = (whole - high).astype(BF16).astype(F32)
        low = whole - high - mid
        three = jnp.where(line == 0, high, jnp.where(line == 1, mid, jnp.where(line == 2, low, 0.0)))
        for i in range(2):
            od_snd[2 * k + i, 64:80, :] = three.astype(BF16)
    own_copies[2].start()
    for slot, dev in column[1:]:
        send(od_snd.at[slot], od.at[own_slot], ro.at[own_slot], dev)

    def row_step(k, waiting):
        row = row_of(k)

        @pl.when(row < y)
        def _():
            step(doc_keys(row * 2), s1, None, s2, doc_vals(waiting))
            step(doc_keys(row * 2 + 1), s2, None, s1, doc_vals(row * 2))

        return jnp.where(row < y, row * 2 + 1, waiting)

    hist.wait_first(far_below)
    hist.send_first(far_below, up)
    hist.wait_second(far_above)
    hist.send_second(far_above, down)
    hist.wait_second(far_below)
    hist.send(far_below, sib)
    hist.wait_first(far_above)
    hist.send(far_above, sib)
    waiting = lax.fori_loop(1, 3, row_step, y * 2)
    for x in range(2):
        b = seq_at(2, x)
        hist.wait_first(b)
        hist.wait_second(b)
        hist.send(b, sib)

    def hist_pair(a, b, vals_t):
        hist.wait_sib(a)
        hist.wait_sib(b)
        step(hist_keys(a), s1, hist_mask(a), s2, vals_t)
        step(hist_keys(b), s2, hist_mask(b), s1, hist_vals(a))


    owners = [owner_ref[chip * 4 + i] for i in range(4)]
    rows_owner = jnp.concatenate([jnp.full((16, 128), o, jnp.int32) for o in owners], axis=0)
    lane = (lax.broadcasted_iota(jnp.int32, (16, 128), 1) >> 4) & 3
    lane_owner = jnp.where(
        lane == 0, owners[0], jnp.where(lane == 1, owners[1], jnp.where(lane == 2, owners[2], owners[3]))
    )
    which = jnp.concatenate([rows_owner, lane_owner], axis=0) == 0
    own_copies[2].wait()
    passed = []
    for k in (0, 1, 7, 2, 6, 3, 5, 4):
        h = (rep + k) % 8
        for g in range(2):
            slot = (grp + g) % 2 * 8 + h
            if k + g > 0:
                arrived(od.at[slot], ro.at[slot])
        chosen = jnp.where(which, od[h].astype(F32), od[8 + h].astype(F32))
        oc[h] = chosen.astype(BF16)
        copy = pltpu.make_async_remote_copy(
            src_ref=oc.at[h],
            dst_ref=of.at[chip],
            send_sem=pass_sem.at[k],
            recv_sem=rf.at[chip],
            device_id={"seq": h * 2 + core},
            device_id_type=MESH,
        )
        passed.append((h, copy))

        @pl.when(h != chip)
        def _(copy=copy):
            copy.start()

    of[chip] = oc[chip]

    waiting = row_step(3, waiting)
    hist_pair(y, (y + 3) % 4, doc_vals(waiting))
    hist_pair((y + 1) % 4, row, hist_vals((y + 3) % 4))
    weigh(s2, hist_vals(row), mrun[...], pre_state)
    total = jnp.sum(tot[...], axis=0, keepdims=True)
    for h in range(8):
        cols = slice(h * 256, (h + 1) * 256)
        o = acc[:, cols] / total[:, cols]
        pre_o[:, h * 128 : (h + 1) * 128] = o.T.astype(BF16)
    pre_copy = pltpu.make_async_copy(pre_o, pre_out, out_sem.at[0])
    pre_copy.start()

    loads[8].wait()
    loads[9].wait()
    new_k = kn[...].astype(F32).reshape(128, 128).astype(BF16)
    new_v = vn[...].astype(F32).reshape(128, 128).astype(BF16)
    arrived(o_sib, rx.at[3])
    arrived(l_sib, rx.at[4])
    for j, _ in plane[1:]:
        arrived(of.at[j], rf.at[j])
    sums = [jnp.sum(of[j, 64:80, :].astype(F32), axis=0, keepdims=True) for j in range(8)]
    lt[...] = jnp.concatenate(sums * 16, axis=0).T
    levels = lt[pl.ds(pl.multiple_of(rep % 2 * 64, 64), 64), :]
    for c in range(4):
        rows = slice(c * 128, (c + 1) * 128)
        l_doc = jnp.concatenate(
            [jnp.broadcast_to(levels[:, j : j + 1], (64, 128)) for j in (2 * c, 2 * c + 1)], axis=0
        )
        o_doc = jnp.concatenate([of[j, 0:64, :].astype(F32) for j in (2 * c, 2 * c + 1)], axis=0)
        s = lax.dot_general(q_own[rows, :], new_k, NT, preferred_element_type=F32)
        line = c * 128 + lax.broadcasted_iota(jnp.int32, (128, 128), 0)
        col = lax.broadcasted_iota(jnp.int32, (128, 128), 1)
        seen = ((line >> 4) == (col >> 2)) & ((col & 3) <= ((line >> 2) & 3))
        s = jnp.where(seen, s, LOW)
        m = jnp.max(s, axis=1, keepdims=True)
        top = jnp.maximum(jnp.maximum(l_doc, l_own[rows, :]), jnp.maximum(l_sib[rows, :], m))
        p = jnp.where(seen, jnp.exp2(s - top), 0.0)
        w_doc = jnp.exp2(l_doc - top)
        w_own = jnp.exp2(l_own[rows, :] - top)
        w_sib = jnp.exp2(l_sib[rows, :] - top)
        o = lax.dot_general(p.astype(BF16), new_v, NN, preferred_element_type=F32)
        o = o + w_doc * o_doc + w_own * o_own[rows, :] + w_sib * o_sib[rows, :].astype(F32)
        weight = jnp.sum(p, axis=1, keepdims=True) + w_doc + w_own + w_sib
        dec_o[rows, :] = (o / weight).astype(BF16)
    dec_copy = pltpu.make_async_copy(dec_o, dec_out, out_sem.at[1])
    dec_copy.start()
    for c in sends:
        c.wait_send()
    for h, copy in passed:

        @pl.when(h != chip)
        def _(copy=copy):
            copy.wait_send()

    pre_copy.wait()
    dec_copy.wait()


def local(
    pre_query,
    history_key,
    history_value,
    document_key,
    document_value,
    stretch_start,
    decode_query,
    cached_row_keys,
    cached_row_values,
    cache_lengths,
    doc_owner,
    decode_key,
    decode_value,
):
    dec_q = decode_query.reshape(512, HEAD)
    smem = pl.BlockSpec(memory_space=pltpu.SMEM)
    hbm = pl.BlockSpec(memory_space=pl.ANY)

    def vm(shape, dtype):
        return pltpu.VMEM(shape, dtype)

    pre, dec = pl.pallas_call(
        kernel,
        out_shape=(
            jax.ShapeDtypeStruct((256, 1024), BF16),
            jax.ShapeDtypeStruct((512, 128), BF16),
        ),
        in_specs=[hbm, hbm, hbm, hbm, hbm, smem, hbm, hbm, hbm, smem, smem, hbm, hbm],
        out_specs=(hbm, hbm),
        scratch_shapes=[
            vm((16, 768, 128), BF16),
            vm((384, 128), BF16),
            vm((2048, 128), BF16),
            vm((256, 1024), BF16),
            vm((256, 1024), BF16),
            vm((512, 128), BF16),
            vm((512, 128), BF16),
            vm((32, 256, 128), BF16),
            vm((32, 256, 128), BF16),
            vm((32, 4, 128), BF16),
            vm((32, 4, 128), BF16),
            vm((512, 128), F32),
            vm((512, 128), F32),
            vm((512, 128), BF16),
            vm((512, 128), F32),
            vm((512, 128), BF16),
            vm((512, 128), F32),
            vm((1024, 128), BF16),
            vm((16, 80, 128), BF16),
            vm((16, 80, 128), BF16),
            vm((8, 80, 128), BF16),
            vm((8, 80, 128), BF16),
            vm((128, 128), F32),
            vm((8, 64, 128), BF16),
            vm((512, 128), BF16),
            vm((512, 2048), F32),
            vm((512, 2048), F32),
            vm((512, 1024), F32),
            vm((512, 1024), F32),
            vm((128, 2048), F32),
            vm((8, 2048), F32),
            vm((8, 2048), F32),
            vm((8, 2048), F32),
            vm((128, 1024), F32),
            vm((8, 1024), F32),
            vm((8, 1024), F32),
            vm((8, 1024), F32),
            pltpu.SemaphoreType.DMA((10,)),
            pltpu.SemaphoreType.DMA((2,)),
            pltpu.SemaphoreType.DMA((96,)),
            pltpu.SemaphoreType.DMA((16,)),
            pltpu.SemaphoreType.DMA((16,)),
            pltpu.SemaphoreType.DMA((16,)),
            pltpu.SemaphoreType.DMA((16,)),
            pltpu.SemaphoreType.DMA((9,)),
            pltpu.SemaphoreType.DMA((8,)),
            pltpu.SemaphoreType.DMA((16,)),
            pltpu.SemaphoreType.DMA((16,)),
            pltpu.SemaphoreType.DMA((8,)),
            pltpu.SemaphoreType.DMA((3,)),
            pltpu.SemaphoreType.DMA((8,)),
        ],
        compiler_params=pltpu.CompilerParams(
            collective_id=0, has_side_effects=True, vmem_limit_bytes=56 * 1024 * 1024
        ),
        name="attention",
    )(
        pre_query[0],
        history_key[0],
        history_value[0],
        document_key[0],
        document_value[0],
        stretch_start,
        dec_q,
        cached_row_keys.reshape(32, 256, HEAD),
        cached_row_values.reshape(32, 256, HEAD),
        cache_lengths,
        doc_owner,
        decode_key,
        decode_value,
    )
    return pre[None], dec.reshape(32, 4, 512)


def solution(mesh):
    placed = (
        P("grp", "seq", "rep"),
        P("grp", "seq", "rep"),
        P("grp", "seq", "rep"),
        P("grp", "seq", "rep"),
        P("grp", "seq", "rep"),
        P("grp"),
        P(("grp", "rep"), None, "seq"),
        P(("grp", "rep"), "seq", None, None),
        P(("grp", "rep"), "seq", None, None),
        P(("grp", "rep")),
        P(("grp", "rep")),
        P(("grp", "rep"), None, None),
        P(("grp", "rep"), None, None),
    )
    return jax.shard_map(
        local,
        mesh=mesh,
        in_specs=placed,
        out_specs=(P("grp", "seq", "rep"), P(("grp", "rep"), None, "seq")),
        check_vma=False,
    )
```
